256 devices in a mesh: batch: 8 (over x_hi, y), frame: 32 (over z, x_lo, core).
Axes of the slice: x: 4 (x_hi: 2, x_lo: 2; x = x_hi * 2 + x_lo), y: 4, z: 8, core: 2. Of those that a mesh axis runs over, the one named last changes fastest.
Arguments:
- tokens: bfloat16 [256, 128, 1152], P(('batch', 'frame')), parts along dimension 0, may hold values from -6 to 6
- anchor: int32 [8], P('batch'), parts along dimension 0, may hold values from 0 to 31
- positions: int32 [256], P('batch'), parts along dimension 0, may hold values from 0 to 1023
- w_spatial: bfloat16 [4, 1152, 1152], P(None, 'frame')
- w_temporal: bfloat16 [4, 1152, 1152], P(None, 'frame')
- mod_shift: float32 [16, 1152], P('batch'), parts along dimension 0, may hold values from -3 to 3
- mod_scale: float32 [16, 1152], P('batch'), parts along dimension 0, may hold values from -1.5 to 1.5
- mod_gate: float32 [16, 1152], P('batch'), parts along dimension 0, may hold values from 0.25 to 1.75
Outputs:
- result: bfloat16 [256, 128, 1152], P(('batch', 'frame')), parts along dimension 0
The draws below stay inside these ranges and needn't reach their ends.
There are 8 independent parts, one for each index of `batch`. The reference program is written for one: setup_inputs(seed, part) draws one part's arguments, and reference() takes and returns one part's arrays. A program takes and returns all parts, laid end to end along the dimension named above; an argument that names none is the same for every part. Nothing has to cross between parts.
All inputs are finite; a program needn't handle non-finite values.
Results may differ from the reference program's by a relative error of at most 0.014.
Values may be sent and summed in bfloat16 or wider, within the bound.
No kernel may reach another device: no remote copies, remote signals or barrier semaphores. Data moves between devices by JAX's collectives and lax.ppermute only.
A program may use at most 128 MiB of HBM per device.

```python
import math
import jax
import jax.numpy as jnp
from jax import lax

D = 1152
HEADS = 16
TOK = 128
FRAMES = 32


def build_stack(query_w, key_w, value_base, out_base, model_width):
    spread_value = (2.0 / model_width) ** 0.5
    return jnp.stack([query_w, key_w, value_base * spread_value, out_base * model_width ** (-0.5)]).astype(jnp.bfloat16)


def draw_w_spatial(key, part):
    key = jax.random.fold_in(key, 11)
    spread_value = (2.0 / D) ** 0.5
    normal_base = jax.random.normal(key, (4, D, D), jnp.float32)
    query_w = normal_base[0] * spread_value
    key_w = normal_base[1] * spread_value
    return build_stack(query_w, key_w, normal_base[2], normal_base[3], D)


def draw_w_temporal(key, part):
    key = jax.random.fold_in(key, 13)
    spread_value = (2.0 / D) ** 0.5
    normal_base = jax.random.normal(key, (4, D, D), jnp.float32)
    query_w = normal_base[0] * spread_value
    key_w = normal_base[1] * spread_value
    return build_stack(query_w, key_w, normal_base[2], normal_base[3], D)


def plant(values, own_key, smallest, high):
    index_at = [jax.random.randint(jax.random.fold_in(own_key, axis), (), 0, length) for axis, length in enumerate(values.shape)]
    main_axis = values.shape.index(max(values.shape))
    neighbour = index_at[:main_axis] + [(index_at[main_axis] + 1) % values.shape[main_axis]] + index_at[main_axis + 1:]
    return values.at[tuple(index_at)].set(smallest).at[tuple(neighbour)].set(high)


def block_scale(stream_key, shape, cuts, low, high):
    factor_of = 1.0
    for dim, blocks in cuts:
        heights = jax.random.uniform(jax.random.fold_in(jax.random.fold_in(stream_key, 6), dim), (blocks,), jnp.float32, low / len(cuts), high / len(cuts))
        factor_of = factor_of * jnp.repeat(jnp.exp(heights), shape[dim] // blocks).reshape((-1,) + (1,) * (len(shape) - 1 - dim))
    return factor_of


def centred(key, extent, spread, most, cuts=(), held_as=jnp.bfloat16):
    array = spread * jax.random.normal(key, extent, jnp.float32)
    if cuts:
        array = array * block_scale(key, extent, cuts, -0.22, 0.18)
    return jnp.clip(array, -most, most).astype(held_as)


def setup_inputs(seed: int = 0, part: int = 0) -> dict:
    arg_keys = jax.random.split(jax.random.key(seed), 9)
    own_keys = jax.random.split(jax.random.fold_in(arg_keys[8], part), 9)
    return {
        "tokens": centred(own_keys[0], (FRAMES, TOK, D), 1.0, 6.0, ((0, 32),)),
        "anchor": jax.random.randint(own_keys[1], (1,), 0, FRAMES).astype(jnp.int32),
        "positions": plant(jax.random.randint(own_keys[2], (FRAMES,), 0, 1024), jax.random.fold_in(own_keys[2], 1), 0, 1023).astype(jnp.int32),
        "w_spatial": draw_w_spatial(jax.random.fold_in(arg_keys[8], 71), part),
        "w_temporal": draw_w_temporal(jax.random.fold_in(arg_keys[8], 71), part),
        "mod_shift": centred(own_keys[5], (2, D), 0.5, 3.0, (), jnp.float32),
        "mod_scale": centred(own_keys[6], (2, D), 0.3, 1.5, (), jnp.float32),
        "mod_gate": jnp.clip(1.0 + 0.15 * jax.random.normal(own_keys[7], (2, D), jnp.float32), 0.25, 1.75),
    }


def modulated_norm(inputs, shift_row, scale_row):
    values = inputs.astype(jnp.float32)
    row_mean = lax.optimization_barrier(jnp.mean(values, axis=-1, keepdims=True))
    centered = values - row_mean
    variance = lax.optimization_barrier(jnp.mean(centered * centered, axis=-1, keepdims=True))
    return (centered * lax.rsqrt(variance + 1e-06) * (1.0 + scale_row) + shift_row).astype(jnp.bfloat16)

def rotate_frames(projected, frame_pos, head_count):
    lead = projected.shape[:-1]
    model_width = projected.shape[-1]
    head_size = model_width // head_count
    half_size = head_size // 2
    split_heads = projected.reshape(lead + (head_count, head_size))
    freqs = 10000.0 ** (-jnp.arange(half_size, dtype=jnp.float32) / half_size)
    angles = frame_pos.astype(jnp.float32)[:, None] * freqs[None, :]
    angles = angles.reshape((angles.shape[0],) + (1,) * (len(lead) - 1) + (1, half_size))
    cosine = jnp.cos(angles)
    sine = jnp.sin(angles)
    front_half = split_heads[..., :half_size]
    back_half = split_heads[..., half_size:]
    turned = jnp.concatenate([front_half * cosine - back_half * sine, back_half * cosine + front_half * sine], axis=-1)
    return turned.reshape(lead + (model_width,))

def reference(tokens, anchor, positions, w_spatial, w_temporal, mod_shift, mod_scale, mod_gate):
    frame_count, seq_len, model_width = tokens.shape
    head_size = model_width // HEADS
    flat = modulated_norm(tokens, mod_shift[0], mod_scale[0]).reshape(frame_count * seq_len, model_width)
    projected = [jnp.dot(flat, w_spatial[matrix_index], preferred_element_type=jnp.float32).astype(jnp.bfloat16).reshape(frame_count, seq_len, model_width) for matrix_index in range(3)]
    queries, key_rows, value_rows = projected
    anchor_keys = lax.dynamic_index_in_dim(key_rows, anchor[0], 0, keepdims=False)
    anchor_values = lax.dynamic_index_in_dim(value_rows, anchor[0], 0, keepdims=False)

    def frame_attention(operands):
        frame_q, frame_k, frame_v = operands
        all_keys = jnp.concatenate([frame_k, anchor_keys], axis=0).astype(jnp.float32).reshape(2 * seq_len, HEADS, head_size)
        all_values = jnp.concatenate([frame_v, anchor_values], axis=0).astype(jnp.float32).reshape(2 * seq_len, HEADS, head_size)
        query_heads = frame_q.astype(jnp.float32).reshape(seq_len, HEADS, head_size)
        scores = jnp.einsum('she,the->hst', query_heads, all_keys) / math.sqrt(head_size)
        weights = jax.nn.softmax(scores, axis=-1).astype(jnp.bfloat16)
        mixed = jnp.einsum('hst,the->she', weights.astype(jnp.float32), all_values)
        return mixed.astype(jnp.bfloat16).reshape(seq_len, model_width)
    attended = lax.map(frame_attention, (queries, key_rows, value_rows))
    spatial_out = jnp.dot(attended.reshape(frame_count * seq_len, model_width), w_spatial[3], preferred_element_type=jnp.float32)
    hidden = (tokens.astype(jnp.float32).reshape(frame_count * seq_len, model_width) + mod_gate[0] * spatial_out).astype(jnp.bfloat16)
    second = modulated_norm(hidden, mod_shift[1], mod_scale[1])
    temporal_q = jnp.dot(second, w_temporal[0], preferred_element_type=jnp.float32).reshape(frame_count, seq_len, model_width)
    temporal_k = jnp.dot(second, w_temporal[1], preferred_element_type=jnp.float32).reshape(frame_count, seq_len, model_width)
    temporal_v = jnp.dot(second, w_temporal[2], preferred_element_type=jnp.float32).astype(jnp.bfloat16)
    temporal_q = rotate_frames(temporal_q, positions, HEADS).astype(jnp.bfloat16)
    temporal_k = rotate_frames(temporal_k, positions, HEADS).astype(jnp.bfloat16)
    split = (frame_count, seq_len, HEADS, head_size)
    scores = jnp.einsum('fshe,gshe->shfg', temporal_q.astype(jnp.float32).reshape(split), temporal_k.astype(jnp.float32).reshape(split)) / math.sqrt(head_size)
    weights = jax.nn.softmax(scores, axis=-1).astype(jnp.bfloat16)
    mixed = jnp.einsum('shfg,gshe->fshe', weights.astype(jnp.float32), temporal_v.astype(jnp.float32).reshape(split))
    mixed = mixed.astype(jnp.bfloat16).reshape(frame_count * seq_len, model_width)
    temporal_out = jnp.dot(mixed, w_temporal[3], preferred_element_type=jnp.float32)
    result = hidden.astype(jnp.float32) + mod_gate[1] * temporal_out
    return result.astype(jnp.bfloat16).reshape(frame_count, seq_len, model_width)
```

```python
import math

import jax
import jax.numpy as jnp
from jax import lax
from jax.experimental import pallas as pl
from jax.experimental.pallas import tpu as pltpu
from jax.sharding import PartitionSpec as P

HEADS = 16
D = 1152
HALF = D // 2
HEAD = D // HEADS
PAD = 640
TOK = 128
FRAMES = 32
AXES = ("batch", "frame")
SAME_CORE = [[2 * chip + core for chip in range(16)] for core in range(2)]


def build_perm(partner):
    pairs = []
    for x_hi in range(2):
        for y in range(4):
            for z in range(8):
                for x_lo in range(2):
                    for core in range(2):
                        x2, z2, c2 = partner(2 * x_hi + x_lo, z, core)
                        x2, z2 = x2 % 4, z2 % 8
                        source = (x_hi * 4 + y) * 32 + z * 4 + x_lo * 2 + core
                        target = ((x2 // 2) * 4 + y) * 32 + z2 * 4 + (x2 % 2) * 2 + c2
                        pairs.append((source, target))
    return pairs


CORE = build_perm(lambda x, z, c: (x, z, 1 - c))
X_LO = build_perm(lambda x, z, c: (x ^ 1, z, c))
X_HI = build_perm(lambda x, z, c: (x + 1 if x % 2 else x - 1, z, c))
Z_EVEN = build_perm(lambda x, z, c: (x, z ^ 1, c))
Z_ODD = build_perm(lambda x, z, c: (x, z + 1 if z % 2 else z - 1, c))


def swap(value, pairs):
    return lax.ppermute(value, AXES, pairs)


def modulated_norm(inputs, shift_row, scale_row):
    values = inputs.astype(jnp.float32)
    row_mean = jnp.mean(values, axis=-1, keepdims=True)
    centered = values - row_mean
    variance = jnp.mean(centered * centered, axis=-1, keepdims=True)
    return (centered * lax.rsqrt(variance + 1e-06) * (1.0 + scale_row) + shift_row).astype(
        jnp.bfloat16
    )


def ordered(core, own, other, axis):
    return jnp.where(
        core == 0,
        jnp.concatenate([own, other], axis=axis),
        jnp.concatenate([other, own], axis=axis),
    )


def chip_slabs(weights, core):
    low, high = weights[..., :HALF], weights[..., HALF:]
    own = jnp.where(core == 0, low, high)
    other = jnp.where(core == 0, high, low)
    own = jnp.concatenate([own[0::2], own[1::2]], axis=-1)
    other = jnp.concatenate([other[0::2], other[1::2]], axis=-1)
    got = swap(other, CORE)
    return ordered(core, own, got, 1)


def gather_weights(slabs, z, x, extra=None):
    side = jnp.where(z % 2 == 0, 1, -1)
    full = [jnp.zeros((16, 72, D), jnp.bfloat16) for _ in range(2)]
    extras = []

    def place(which, block, z_at, x_at):
        full[which] = lax.dynamic_update_slice(
            full[which], block[None], ((z_at % 8) * 2 + x_at, 0, 0)
        )

    def arrive(which, block, z_at):
        if which == 0 and extra is not None:
            extras.append((z_at % 8, block[72:]))
            block = block[:72]
        place(which, block, z_at, x)
        place(which, swap(block, X_LO if which == 0 else X_HI), z_at, 1 - x)

    start = [slabs[0], slabs[1]]
    if extra is not None:
        start[0] = jnp.concatenate([start[0], extra], axis=0)
    even = list(start)
    odd = list(start)
    for step in range(4):
        if step == 0:
            for which in range(2):
                arrive(which, start[which], z)
        last = step == 3
        new_even, new_odd = [None, None], [None, None]
        for which in range(2):
            if not last or which == 0:
                new_even[which] = swap(odd[which], Z_EVEN)
            if not last or which == 1:
                new_odd[which] = swap(even[which], Z_ODD)
        even, odd = new_even, new_odd
        for which in range(2):
            if even[which] is not None:
                arrive(which, even[which], z + side * (step + 1))
            if odd[which] is not None:
                arrive(which, odd[which], z - side * (step + 1))
    return [w.reshape(D, D) for w in full], extras


def head_window(head):
    first = head * HEAD
    begin = first // 128 * 128
    end = -(-(first + HEAD) // 128) * 128
    return first, begin, end


def attend(q, k, v, mix_ref, row0, rows, bias):
    for head in range(HEADS // 2):
        first, begin, end = head_window(head)
        lane = lax.broadcasted_iota(jnp.int32, (1, end - begin), 1) + begin
        inside = (lane >= first) & (lane < first + HEAD)
        qw = jnp.where(inside, q[:, begin:end], 0).astype(jnp.bfloat16)
        scores = lax.dot_general(
            qw,
            k[:, begin:end],
            (((1,), (1,)), ((), ())),
            preferred_element_type=jnp.float32,
        ) * (1.0 / math.sqrt(HEAD))
        if bias is not None:
            scores = jnp.where(bias, scores, -1e30)
        top = jnp.max(scores, axis=-1, keepdims=True)
        weight = jnp.exp(scores - top)
        total = jnp.sum(weight, axis=-1, keepdims=True)
        out = jnp.dot(
            weight.astype(jnp.bfloat16), v[:, begin:end], preferred_element_type=jnp.float32
        ) / total
        here = mix_ref[row0 : row0 + rows, begin:end]
        mix_ref[row0 : row0 + rows, begin:end] = jnp.where(inside, out, here)


def spatial_kernel(normed_ref, wqk_ref, wvo_ref, out_ref, q_s, k_s, v_s, mix_s):
    normed = normed_ref[...]
    qk = jnp.dot(normed, wqk_ref[...], preferred_element_type=jnp.float32).astype(jnp.bfloat16)
    v = jnp.dot(normed, wvo_ref[:, :PAD], preferred_element_type=jnp.float32).astype(jnp.bfloat16)
    q_s[...] = qk[: 2 * TOK, :PAD]
    k_s[:, :HALF] = qk[:, HALF:]
    k_s[:, HALF:] = jnp.zeros((3 * TOK, PAD - HALF), jnp.bfloat16)
    v_s[...] = v
    for frame in range(2):
        r0 = frame * TOK
        keys = jnp.concatenate([k_s[r0 : r0 + TOK], k_s[2 * TOK :]], axis=0)
        vals = jnp.concatenate([v_s[r0 : r0 + TOK], v_s[2 * TOK :]], axis=0)
        attend(q_s[r0 : r0 + TOK], keys, vals, mix_s, r0, TOK, None)
    out_ref[...] = mix_s[:, :HALF].astype(jnp.bfloat16)


def temporal_kernel(normed_ref, wqk_ref, wvo_ref, cos_ref, sin_ref, out_ref, mix_s):
    rows = 2 * TOK
    normed = normed_ref[...]
    q = jnp.dot(normed, wqk_ref[:, :PAD], preferred_element_type=jnp.float32)
    k = jnp.dot(normed, wqk_ref[:, 512:], preferred_element_type=jnp.float32)
    k = pltpu.roll(k, PAD - 64, 1)
    v = jnp.dot(normed, wvo_ref[:, :PAD], preferred_element_type=jnp.float32).astype(jnp.bfloat16)
    lane = lax.broadcasted_iota(jnp.int32, (rows, PAD), 1)
    front = lane % HEAD < HEAD // 2
    cos, sin = cos_ref[...], sin_ref[...]

    def rotate(a):
        other = jnp.where(front, pltpu.roll(a, PAD - HEAD // 2, 1), pltpu.roll(a, HEAD // 2, 1))
        return (a * cos + other * sin).astype(jnp.bfloat16)

    q, k = rotate(q), rotate(k)
    place_r = lax.broadcasted_iota(jnp.int32, (rows, rows), 0) // 2 % 8
    place_c = lax.broadcasted_iota(jnp.int32, (rows, rows), 1) // 2 % 8
    attend(q, k, v, mix_s, 0, rows, place_r == place_c)
    out_ref[...] = mix_s[:, :HALF].astype(jnp.bfloat16)


def whole():
    return pl.BlockSpec(memory_space=pltpu.VMEM)


def on_device(tokens, anchor, positions, w_spatial, w_temporal, mod_shift, mod_scale, mod_gate):
    index = lax.axis_index("frame")
    z, x, core = index // 4, index // 2 % 2, index % 2
    root = anchor[0]
    root_z, root_x, root_core = root // 4, root // 2 % 2, root % 2

    s_slabs = chip_slabs(w_spatial, core)
    own = tokens[0]
    other = swap(own, CORE)
    pair = ordered(core, own, other, 0)
    candidate = jnp.where(root_core == core, own, other)
    mine = lax.dynamic_slice_in_dim(candidate, (2 * x + core) * 32, 32, 0)
    theirs = lax.dynamic_slice_in_dim(candidate, (2 * (1 - x) + core) * 32, 32, 0)
    quarter = jnp.where(root_x == x, mine, swap(theirs, X_LO))

    (s_qk, s_vo), quarters = gather_weights(s_slabs, z, x, quarter)
    chosen = jnp.zeros((32, D), jnp.bfloat16)
    for z_at, block in quarters:
        chosen = jnp.where(root_z == z_at, block, chosen)
    half = jnp.concatenate([chosen, swap(chosen, X_LO)], axis=0)
    anchor_rows = jnp.concatenate([half, swap(half, CORE)], axis=0)

    normed = modulated_norm(
        jnp.concatenate([pair, anchor_rows], axis=0), mod_shift[0], mod_scale[0]
    )
    mix = pl.pallas_call(
        spatial_kernel,
        out_shape=jax.ShapeDtypeStruct((2 * TOK, HALF), jnp.bfloat16),
        in_specs=[whole()] * 3,
        out_specs=whole(),
        scratch_shapes=[
            pltpu.VMEM((2 * TOK, PAD), jnp.bfloat16),
            pltpu.VMEM((3 * TOK, PAD), jnp.bfloat16),
            pltpu.VMEM((3 * TOK, PAD), jnp.bfloat16),
            pltpu.VMEM((2 * TOK, PAD), jnp.float32),
        ],
        compiler_params=pltpu.CompilerParams(vmem_limit_bytes=32 * 2**20),
        name="spatial",
    )(normed, s_qk, s_vo)
    mixed = ordered(core, mix, swap(mix, CORE), 1)
    spatial_out = jnp.dot(mixed, s_vo[:, HALF:], preferred_element_type=jnp.float32)

    def own_half(a):
        return jnp.where(core == 0, a[..., :HALF], a[..., HALF:])

    hidden = (own_half(pair).astype(jnp.float32) + own_half(mod_gate[0]) * spatial_out).astype(
        jnp.bfloat16
    )
    t_slabs = chip_slabs(w_temporal, core)
    (t_qk, t_vo), _ = gather_weights(t_slabs, z, x)

    blocks = hidden.reshape(2, 16, 8, HALF).transpose(1, 2, 0, 3).reshape(16, 8, D)
    moved = lax.all_to_all(
        blocks, "frame", split_axis=0, concat_axis=0, axis_index_groups=SAME_CORE, tiled=True
    )
    there = swap(moved, CORE)
    moved = moved.reshape(2 * TOK, HALF)
    rows = ordered(core, moved, there.reshape(2 * TOK, HALF), 1)
    normed_rows = modulated_norm(rows, mod_shift[1], mod_scale[1])

    half_size = HEAD // 2
    freqs = 10000.0 ** (-jnp.arange(half_size, dtype=jnp.float32) / half_size)
    angles = positions.astype(jnp.float32)[:, None] * freqs[None, :]
    cosine, sine = jnp.cos(angles), jnp.sin(angles)

    def spread(first, second):
        table = jnp.tile(jnp.concatenate([first, second], axis=1), (1, HEADS // 2))
        table = jnp.pad(table, ((0, 0), (0, PAD - HALF)))
        table = jnp.broadcast_to(table.reshape(16, 1, 2, PAD), (16, 8, 2, PAD))
        return table.reshape(2 * TOK, PAD)

    t_mix = pl.pallas_call(
        temporal_kernel,
        out_shape=jax.ShapeDtypeStruct((2 * TOK, HALF), jnp.bfloat16),
        in_specs=[whole()] * 5,
        out_specs=whole(),
        scratch_shapes=[pltpu.VMEM((2 * TOK, PAD), jnp.float32)],
        compiler_params=pltpu.CompilerParams(vmem_limit_bytes=32 * 2**20),
        name="temporal",
    )(normed_rows, t_qk, t_vo, spread(cosine, cosine), spread(-sine, sine))
    t_mixed = ordered(core, t_mix, swap(t_mix, CORE), 1)
    temporal_out = jnp.dot(t_mixed, t_vo[:, HALF:], preferred_element_type=jnp.float32)
    result = (moved.astype(jnp.float32) + own_half(mod_gate[1]) * temporal_out).astype(
        jnp.bfloat16
    )
    back = lax.all_to_all(
        result.reshape(16, 8, D),
        "frame",
        split_axis=0,
        concat_axis=0,
        axis_index_groups=SAME_CORE,
        tiled=True,
    ).reshape(TOK, 2, HALF)
    keep = jnp.where(core == 0, back[:, 0], back[:, 1])
    give = jnp.where(core == 0, back[:, 1], back[:, 0])
    return ordered(core, keep, swap(give, CORE), 1)[None]


def solution(mesh):
    placed = (
        P(("batch", "frame"), None, None),
        P("batch"),
        P("batch"),
        P(None, "frame", None),
        P(None, "frame", None),
        P("batch", None),
        P("batch", None),
        P("batch", None),
    )
    return jax.shard_map(
        on_device,
        mesh=mesh,
        in_specs=placed,
        out_specs=P(("batch", "frame"), None, None),
        check_vma=False,
    )
```

```python
import math

import jax
import jax.numpy as jnp
from jax import lax
from jax.experimental import pallas as pl
from jax.experimental.pallas import tpu as pltpu
from jax.sharding import PartitionSpec as P

HEADS = 16
D = 1152
HALF = D // 2
HEAD = D // HEADS
PAD = 640
TOK = 128
FRAMES = 32
AXES = ("batch", "frame")
SAME_X = [[4 * z + 2 * x + core for z in range(8) for core in range(2)] for x in range(2)]


def build_perm(partner):
    pairs = []
    for x_hi in range(2):
        for y in range(4):
            for z in range(8):
                for x_lo in range(2):
                    for core in range(2):
                        x2, z2, c2 = partner(2 * x_hi + x_lo, z, core)
                        x2, z2 = x2 % 4, z2 % 8
                        source = (x_hi * 4 + y) * 32 + z * 4 + x_lo * 2 + core
                        target = ((x2 // 2) * 4 + y) * 32 + z2 * 4 + (x2 % 2) * 2 + c2
                        pairs.append((source, target))
    return pairs


CORE = build_perm(lambda x, z, c: (x, z, 1 - c))
X_LO = build_perm(lambda x, z, c: (x ^ 1, z, c))
Z_BITS = [build_perm(lambda x, z, c, bit=bit: (x, z ^ bit, c)) for bit in (1, 2, 4)]


def swap(value, pairs):
    return lax.ppermute(value, AXES, pairs)


def modulated_norm(inputs, shift_row, scale_row):
    values = inputs.astype(jnp.float32)
    row_mean = jnp.mean(values, axis=-1, keepdims=True)
    centered = values - row_mean
    variance = jnp.mean(centered * centered, axis=-1, keepdims=True)
    return (centered * lax.rsqrt(variance + 1e-06) * (1.0 + scale_row) + shift_row).astype(
        jnp.bfloat16
    )


def ordered(place, own, other, axis):
    return jnp.where(
        place == 0,
        jnp.concatenate([own, other], axis=axis),
        jnp.concatenate([other, own], axis=axis),
    )


def regroup(a, roll):
    width = a.shape[-1]
    spot = lax.broadcasted_iota(jnp.int32, a.shape, a.ndim - 1) % 144
    ahead = roll(a, width - 36, a.ndim - 1)
    behind = roll(a, 36, a.ndim - 1)
    return jnp.where(
        (spot >= 36) & (spot < 72), ahead, jnp.where((spot >= 72) & (spot < 108), behind, a)
    )


def halves(a, x):
    low, high = a[..., :HALF], a[..., HALF:]
    return jnp.where(x == 0, low, high), jnp.where(x == 0, high, low)


def gather_rows(slab):
    return lax.all_gather(slab, "frame", axis_index_groups=SAME_X)


def spatial_slab(weights, x):
    own, other = halves(weights, x)
    own = jnp.concatenate([own[0::2], own[1::2]], axis=-1)
    other = jnp.concatenate([other[0::2], other[1::2]], axis=-1)
    return ordered(x, own, swap(other, X_LO), 1).reshape(144, D)


def temporal_slab(weights, x):
    own, other = halves(weights[:3], x)
    own = jnp.concatenate([own[0], own[1], own[2], weights[3]], axis=-1)
    other = jnp.concatenate([other[0], other[1], other[2], weights[3]], axis=-1)
    got = swap(other, X_LO)
    v = 2 * HALF
    o = 3 * HALF
    return jnp.concatenate(
        [
            ordered(x, own[:, :v], got[:, :v], 0),
            ordered(x, own[:, v:o], got[:, v:o], 1),
            ordered(x, own[:, o:], got[:, o:], 0),
        ],
        axis=0,
    )


def head_window(head):
    first = head * HEAD
    begin = first // 128 * 128
    end = -(-(first + HEAD) // 128) * 128
    return first, begin, end


def attend(q, k, v, mix_ref, row0, rows, bias):
    for head in range(HEADS // 2):
        first, begin, end = head_window(head)
        lane = lax.broadcasted_iota(jnp.int32, (1, end - begin), 1) + begin
        inside = (lane >= first) & (lane < first + HEAD)
        qw = jnp.where(inside, q[:, begin:end], 0).astype(jnp.bfloat16)
        scores = lax.dot_general(
            qw,
            k[:, begin:end],
            (((1,), (1,)), ((), ())),
            preferred_element_type=jnp.float32,
        ) * (1.0 / math.sqrt(HEAD))
        if bias is not None:
            scores = jnp.where(bias, scores, -1e30)
        top = jnp.max(scores, axis=-1, keepdims=True)
        weight = jnp.exp(scores - top)
        total = jnp.sum(weight, axis=-1, keepdims=True)
        out = jnp.dot(
            weight.astype(jnp.bfloat16), v[:, begin:end], preferred_element_type=jnp.float32
        ) / total
        here = mix_ref[row0 : row0 + rows, begin:end]
        mix_ref[row0 : row0 + rows, begin:end] = jnp.where(inside, out, here)


def spatial_kernel(normed_ref, wqk_ref, wvo_ref, out_ref, q_s, k_s, v_s, mix_s):
    normed = normed_ref[...]
    qk = jnp.dot(normed, wqk_ref[...], preferred_element_type=jnp.float32).astype(jnp.bfloat16)
    v = jnp.dot(normed, wvo_ref[:, :PAD], preferred_element_type=jnp.float32).astype(jnp.bfloat16)
    q_s[...] = qk[: 2 * TOK, :PAD]
    k_s[:, :HALF] = qk[:, HALF:]
    k_s[:, HALF:] = jnp.zeros((3 * TOK, PAD - HALF), jnp.bfloat16)
    v_s[...] = v
    for frame in range(2):
        r0 = frame * TOK
        keys = jnp.concatenate([k_s[r0 : r0 + TOK], k_s[2 * TOK :]], axis=0)
        vals = jnp.concatenate([v_s[r0 : r0 + TOK], v_s[2 * TOK :]], axis=0)
        attend(q_s[r0 : r0 + TOK], keys, vals, mix_s, r0, TOK, None)
    out_ref[...] = regroup(mix_s[...], pltpu.roll)[:, :HALF].astype(jnp.bfloat16)


def temporal_kernel(
    rows_ref, shift_ref, scale_ref, wqk_ref, wv_ref, cos_ref, sin_ref, out_ref, mix_s
):
    rows = 2 * TOK
    values = rows_ref[...].astype(jnp.float32)
    centered = values - jnp.mean(values, axis=-1, keepdims=True)
    variance = jnp.mean(centered * centered, axis=-1, keepdims=True)
    normed = centered * lax.rsqrt(variance + 1e-06) * (1.0 + scale_ref[...]) + shift_ref[...]
    normed = regroup(normed, pltpu.roll).astype(jnp.bfloat16)
    q = jnp.dot(normed, wqk_ref[:, :PAD], preferred_element_type=jnp.float32)
    k = jnp.dot(normed, wqk_ref[:, 512:], preferred_element_type=jnp.float32)
    k = pltpu.roll(k, PAD - 64, 1)
    v = jnp.dot(normed, wv_ref[...], preferred_element_type=jnp.float32).astype(jnp.bfloat16)
    v = jnp.concatenate([v, jnp.zeros((rows, PAD - HALF), jnp.bfloat16)], axis=1)
    lane = lax.broadcasted_iota(jnp.int32, (rows, PAD), 1)
    front = lane % HEAD < HEAD // 2
    cos, sin = cos_ref[...], sin_ref[...]

    def rotate(a):
        other = jnp.where(front, pltpu.roll(a, PAD - HEAD // 2, 1), pltpu.roll(a, HEAD // 2, 1))
        return (a * cos + other * sin).astype(jnp.bfloat16)

    q, k = rotate(q), rotate(k)
    place_r = lax.broadcasted_iota(jnp.int32, (rows, rows), 0) % 8
    place_c = lax.broadcasted_iota(jnp.int32, (rows, rows), 1) % 8
    attend(q, k, v, mix_s, 0, rows, place_r == place_c)
    out_ref[...] = regroup(mix_s[...], pltpu.roll)[:, :HALF].astype(jnp.bfloat16)


def whole():
    return pl.BlockSpec(memory_space=pltpu.VMEM)


def on_device(tokens, anchor, positions, w_spatial, w_temporal, mod_shift, mod_scale, mod_gate):
    index = lax.axis_index("frame")
    z, x, core = index // 4, index // 2 % 2, index % 2
    root = anchor[0]
    root_z, root_x, root_core = root // 4, root // 2 % 2, root % 2

    s_full = gather_rows(spatial_slab(w_spatial, x))

    own = tokens[0]
    candidate = jnp.where(root_core == core, own, swap(own, CORE))
    mine = lax.dynamic_slice_in_dim(candidate, (2 * x + core) * 32, 32, 0)
    theirs = lax.dynamic_slice_in_dim(candidate, (2 * (1 - x) + core) * 32, 32, 0)
    quarter = jnp.where(root_x == x, mine, swap(theirs, X_LO))
    for bit, pairs in enumerate(Z_BITS):
        same = (z >> bit) % 2 == (root_z >> bit) % 2
        quarter = jnp.where(same, quarter, swap(quarter, pairs))
    half = jnp.concatenate([quarter, swap(quarter, X_LO)], axis=0)
    anchor_rows = jnp.concatenate([half, swap(half, CORE)], axis=0)

    pair = ordered(x, own, swap(own, X_LO), 0)
    normed = modulated_norm(
        jnp.concatenate([pair, anchor_rows], axis=0), mod_shift[0], mod_scale[0]
    )
    normed = regroup(normed, jnp.roll)
    t_slab, normed = lax.optimization_barrier((temporal_slab(w_temporal, x), normed))
    t_full = gather_rows(t_slab)

    s_qk = s_full[:, :72].reshape(D, D)
    s_vo = s_full[:, 72:].reshape(D, D)
    mix = pl.pallas_call(
        spatial_kernel,
        out_shape=jax.ShapeDtypeStruct((2 * TOK, HALF), jnp.bfloat16),
        in_specs=[whole()] * 3,
        out_specs=whole(),
        scratch_shapes=[
            pltpu.VMEM((2 * TOK, PAD), jnp.bfloat16),
            pltpu.VMEM((3 * TOK, PAD), jnp.bfloat16),
            pltpu.VMEM((3 * TOK, PAD), jnp.bfloat16),
            pltpu.VMEM((2 * TOK, PAD), jnp.float32),
        ],
        compiler_params=pltpu.CompilerParams(vmem_limit_bytes=32 * 2**20),
        name="spatial",
    )(normed, s_qk, s_vo)
    mixed = ordered(x, mix, swap(mix, X_LO), 1)
    spatial_out = jnp.dot(mixed, s_vo[:, HALF:], preferred_element_type=jnp.float32)
    hidden = (
        halves(pair, x)[0].astype(jnp.float32) + halves(mod_gate[0], x)[0] * spatial_out
    ).astype(jnp.bfloat16)

    blocks = hidden.reshape(2, 16, 8, HALF).transpose(1, 2, 0, 3).reshape(16, 8, D)
    moved = lax.all_to_all(
        blocks, "frame", split_axis=0, concat_axis=0, axis_index_groups=SAME_X, tiled=True
    ).reshape(TOK, D)
    there = swap(moved, X_LO)
    rows = jnp.concatenate(
        [
            ordered(x, moved[:, :HALF], there[:, :HALF], 1),
            ordered(x, moved[:, HALF:], there[:, HALF:], 1),
        ],
        axis=0,
    )

    half_size = HEAD // 2
    freqs = 10000.0 ** (-jnp.arange(half_size, dtype=jnp.float32) / half_size)
    by_row = positions.reshape(8, 2, 2).transpose(1, 0, 2).reshape(32)
    angles = by_row.astype(jnp.float32)[:, None] * freqs[None, :]
    cosine, sine = jnp.cos(angles), jnp.sin(angles)

    def spread(first, second):
        table = jnp.tile(jnp.concatenate([first, second], axis=1), (1, HEADS // 2))
        table = jnp.pad(table, ((0, 0), (0, PAD - HALF)))
        return jnp.broadcast_to(table[:, None], (32, 8, PAD)).reshape(2 * TOK, PAD)

    t_qk = t_full[:, :72].reshape(D, D)
    t_v = t_full[:, 72:108].reshape(16, 36, 2, HALF).transpose(0, 2, 1, 3).reshape(D, HALF)
    t_o = t_full[:, 108:].reshape(D, D)
    t_mix = pl.pallas_call(
        temporal_kernel,
        out_shape=jax.ShapeDtypeStruct((2 * TOK, HALF), jnp.bfloat16),
        in_specs=[whole()] * 7,
        out_specs=whole(),
        scratch_shapes=[pltpu.VMEM((2 * TOK, PAD), jnp.float32)],
        compiler_params=pltpu.CompilerParams(vmem_limit_bytes=32 * 2**20),
        name="temporal",
    )(
        rows,
        mod_shift[1:],
        mod_scale[1:],
        t_qk,
        t_v,
        spread(cosine, cosine),
        spread(-sine, sine),
    )
    keep = jnp.where(x == 0, t_mix[:TOK], t_mix[TOK:])
    give = jnp.where(x == 0, t_mix[TOK:], t_mix[:TOK])
    t_mixed = ordered(x, keep, swap(give, X_LO), 1)
    temporal_out = jnp.dot(t_mixed, t_o, preferred_element_type=jnp.float32)
    own_rows = jnp.where(x == 0, rows[:TOK], rows[TOK:])
    result = (own_rows.astype(jnp.float32) + mod_gate[1] * temporal_out).astype(jnp.bfloat16)
    back = lax.all_to_all(
        result.reshape(16, 8, D),
        "frame",
        split_axis=0,
        concat_axis=0,
        axis_index_groups=SAME_X,
        tiled=True,
    )
    return back.reshape(1, TOK, D)


def solution(mesh):
    placed = (
        P(("batch", "frame"), None, None),
        P("batch"),
        P("batch"),
        P(None, "frame", None),
        P(None, "frame", None),
        P("batch", None),
        P("batch", None),
        P("batch", None),
    )
    return jax.shard_map(
        on_device,
        mesh=mesh,
        in_specs=placed,
        out_specs=P(("batch", "frame"), None, None),
        check_vma=False,
    )
```

```python
import math

import jax
import jax.numpy as jnp
from jax import lax
from jax.experimental import pallas as pl
from jax.experimental.pallas import tpu as pltpu
from jax.sharding import PartitionSpec as P

HEADS = 16
D = 1152
HALF = D // 2
HEAD = D // HEADS
PAD = 640
TOK = 128
FRAMES = 32
AXES = ("batch", "frame")
SAME_X = [[4 * z + 2 * x + core for z in range(8) for core in range(2)] for x in range(2)]


def build_perm(partner):
    pairs = []
    for x_hi in range(2):
        for y in range(4):
            for z in range(8):
                for x_lo in range(2):
                    for core in range(2):
                        x2, z2, c2 = partner(2 * x_hi + x_lo, z, core)
                        x2, z2 = x2 % 4, z2 % 8
                        source = (x_hi * 4 + y) * 32 + z * 4 + x_lo * 2 + core
                        target = ((x2 // 2) * 4 + y) * 32 + z2 * 4 + (x2 % 2) * 2 + c2
                        pairs.append((source, target))
    return pairs


CORE = build_perm(lambda x, z, c: (x, z, 1 - c))
X_LO = build_perm(lambda x, z, c: (x ^ 1, z, c))
X_HI = build_perm(lambda x, z, c: (x + 1 if x % 2 else x - 1, z, c))
Z_EVEN = build_perm(lambda x, z, c: (x, z ^ 1, c))
Z_ODD = build_perm(lambda x, z, c: (x, z + 1 if z % 2 else z - 1, c))


def swap(value, pairs):
    return lax.ppermute(value, AXES, pairs)


def modulated_norm(inputs, shift_row, scale_row):
    values = inputs.astype(jnp.float32)
    row_mean = jnp.mean(values, axis=-1, keepdims=True)
    centered = values - row_mean
    variance = jnp.mean(centered * centered, axis=-1, keepdims=True)
    return (centered * lax.rsqrt(variance + 1e-06) * (1.0 + scale_row) + shift_row).astype(
        jnp.bfloat16
    )


def ordered(place, own, other, axis):
    return jnp.where(
        place == 0,
        jnp.concatenate([own, other], axis=axis),
        jnp.concatenate([other, own], axis=axis),
    )


def regroup(a, roll):
    width = a.shape[-1]
    spot = lax.broadcasted_iota(jnp.int32, a.shape, a.ndim - 1) % 144
    ahead = roll(a, width - 36, a.ndim - 1)
    behind = roll(a, 36, a.ndim - 1)
    return jnp.where(
        (spot >= 36) & (spot < 72), ahead, jnp.where((spot >= 72) & (spot < 108), behind, a)
    )


def halves(a, x):
    low, high = a[..., :HALF], a[..., HALF:]
    return jnp.where(x == 0, low, high), jnp.where(x == 0, high, low)


def spatial_slabs(weights, quarter, x):
    own, other = halves(weights, x)
    own = jnp.concatenate([own[i] for i in range(4)], axis=-1)
    other = jnp.concatenate([other[i] for i in range(4)], axis=-1)
    rows = ordered(x, own, swap(other, X_HI), 0)
    extra = quarter.reshape(8, 4, 9, 128).transpose(0, 2, 1, 3).reshape(72, 512)
    return (
        jnp.concatenate([rows[:, :D], extra[:, :256]], axis=1),
        jnp.concatenate([rows[:, D:], extra[:, 256:]], axis=1),
    )


def put(full, block, z_at):
    return lax.dynamic_update_slice(full, block[None], (z_at % 8, 0, 0))


def both_cores(own, other, core):
    full = jnp.stack(
        [jnp.where(core == 0, own, other), jnp.where(core == 0, other, own)], axis=1
    )
    return full.reshape(D, own.shape[-1])


def ring_gather(slabs, z, side):
    full = [put(jnp.zeros((8,) + slab.shape, slab.dtype), slab, z) for slab in slabs]
    even, odd = list(slabs), list(slabs)
    for step in (1, 2, 3):
        for i in range(2):
            even[i], odd[i] = swap(odd[i], Z_EVEN), swap(even[i], Z_ODD)
            full[i] = put(put(full[i], even[i], z + side * step), odd[i], z - side * step)
    full[0] = put(full[0], swap(odd[0], Z_EVEN), z + 4)
    full[1] = put(full[1], swap(even[1], Z_ODD), z + 4)
    return full


def quarter_rows(extra):
    return extra.reshape(-1, 8, 9, 4, 128).transpose(0, 1, 3, 2, 4).reshape(-1, D)


def temporal_slab(weights, x):
    own, other = halves(weights[:3], x)
    pad = jnp.zeros((36, PAD - HALF), weights.dtype)
    own = jnp.concatenate([own[0], own[1], weights[3], own[2], pad], axis=-1)
    other = jnp.concatenate([other[0], other[1], weights[3], other[2], pad], axis=-1)
    return ordered(x, own, swap(other, X_HI), 0)


def head_window(head):
    first = head * HEAD
    begin = first // 128 * 128
    end = -(-(first + HEAD) // 128) * 128
    return first, begin, end


def attend(q, k, v, mix_ref, row0, rows, bias):
    for head in range(HEADS // 2):
        first, begin, end = head_window(head)
        lane = lax.broadcasted_iota(jnp.int32, (1, end - begin), 1) + begin
        inside = (lane >= first) & (lane < first + HEAD)
        qw = jnp.where(inside, q[:, begin:end], 0).astype(jnp.bfloat16)
        scores = lax.dot_general(
            qw,
            k[:, begin:end],
            (((1,), (1,)), ((), ())),
            preferred_element_type=jnp.float32,
        ) * (1.0 / math.sqrt(HEAD))
        if bias is not None:
            scores = jnp.where(bias, scores, -1e30)
        top = jnp.max(scores, axis=-1, keepdims=True)
        weight = jnp.exp(scores - top)
        total = jnp.sum(weight, axis=-1, keepdims=True)
        out = jnp.dot(
            weight.astype(jnp.bfloat16), v[:, begin:end], preferred_element_type=jnp.float32
        ) / total
        here = mix_ref[row0 : row0 + rows, begin:end]
        mix_ref[row0 : row0 + rows, begin:end] = jnp.where(inside, out, here)


def norm_regroup(values, shift, scale):
    centered = values - jnp.mean(values, axis=-1, keepdims=True)
    variance = jnp.mean(centered * centered, axis=-1, keepdims=True)
    normed = centered * lax.rsqrt(variance + 1e-06) * (1.0 + scale) + shift
    return regroup(normed, pltpu.roll).astype(jnp.bfloat16)


def project_kernel(normed_ref, wa_ref, wb_ref, qk_ref, v_ref):
    normed = normed_ref[...]
    qk = jnp.dot(normed, wa_ref[:, :D], preferred_element_type=jnp.float32)
    qk_ref[...] = qk.astype(jnp.bfloat16)
    v = jnp.dot(normed, wb_ref[:, :PAD], preferred_element_type=jnp.float32)
    v_ref[...] = v.astype(jnp.bfloat16)


def spatial_kernel(
    qk_ref, v_ref, anchor_ref, shift_ref, scale_ref, wa_ref, wb_ref, out_ref, mix_s
):
    anchor = norm_regroup(anchor_ref[...].astype(jnp.float32), shift_ref[...], scale_ref[...])
    anchor_k = jnp.dot(anchor, wa_ref[:, 512:D], preferred_element_type=jnp.float32)
    anchor_v = jnp.dot(anchor, wb_ref[:, :PAD], preferred_element_type=jnp.float32).astype(
        jnp.bfloat16
    )
    anchor_k = pltpu.roll(anchor_k, PAD - 64, 1).astype(jnp.bfloat16)
    own_k = pltpu.roll(qk_ref[:, 512:].astype(jnp.float32), PAD - 64, 1).astype(jnp.bfloat16)
    for frame in range(2):
        r0 = frame * TOK
        keys = jnp.concatenate([own_k[r0 : r0 + TOK], anchor_k], axis=0)
        vals = jnp.concatenate([v_ref[r0 : r0 + TOK], anchor_v], axis=0)
        attend(qk_ref[r0 : r0 + TOK, :PAD], keys, vals, mix_s, r0, TOK, None)
    out_ref[...] = regroup(mix_s[...], pltpu.roll)[:, :HALF].astype(jnp.bfloat16)


def mixed_dot(x, own, got, w_ref, column, width):
    def part(side, values):
        rows = pl.ds(pl.multiple_of(side * HALF, HALF), HALF)
        return jnp.dot(
            values, w_ref[rows, column : column + width], preferred_element_type=jnp.float32
        )

    return part(x, own) + part(1 - x, got)


def hidden_kernel(x_ref, own_ref, got_ref, tokens_ref, gate_ref, wb_ref, out_ref):
    added = mixed_dot(x_ref[0], own_ref[...], got_ref[...], wb_ref, 512, PAD)
    added = pltpu.roll(added, PAD - 64, 1)[:, :HALF]
    hidden = (tokens_ref[...].astype(jnp.float32) + gate_ref[...] * added).astype(jnp.bfloat16)
    out_ref[:, :HALF] = hidden[:TOK]
    out_ref[:, HALF:] = hidden[TOK:]


def rows_kernel(x_ref, moved_ref, there_ref, shift_ref, scale_ref, rows_ref, normed_ref):
    x = x_ref[0]
    moved, there = moved_ref[...], there_ref[...]
    low = jnp.where(x == 0, moved, there)
    high = jnp.where(x == 0, there, moved)
    first = jnp.concatenate([low[:, :HALF], high[:, :HALF]], axis=1)
    second = jnp.concatenate([low[:, HALF:], high[:, HALF:]], axis=1)
    own = jnp.where(x == 0, first, second)
    rows_ref[...] = own
    values = jnp.concatenate([own, jnp.where(x == 0, second, first)], axis=0)
    normed_ref[...] = norm_regroup(values.astype(jnp.float32), shift_ref[...], scale_ref[...])


def same_place():
    place_r = lax.broadcasted_iota(jnp.int32, (TOK, 2 * TOK), 0) % 8
    place_c = lax.broadcasted_iota(jnp.int32, (TOK, 2 * TOK), 1) % 8
    return place_r == place_c


def temporal_kernel(
    normed_ref, cos_ref, sin_ref, w_ref, give_ref, q_ref, k_ref, v_ref, mix_s
):
    rows = 2 * TOK
    normed = normed_ref[...]
    lane = lax.broadcasted_iota(jnp.int32, (rows, PAD), 1)
    front = lane % HEAD < HEAD // 2
    cos, sin = cos_ref[...], sin_ref[...]
    q = jnp.dot(normed, w_ref[:, :PAD], preferred_element_type=jnp.float32)
    k = jnp.dot(normed, w_ref[:, 512:D], preferred_element_type=jnp.float32)
    k = pltpu.roll(k, PAD - 64, 1)
    v = jnp.dot(normed, w_ref[:, 2 * D :], preferred_element_type=jnp.float32)
    v = v.astype(jnp.bfloat16)

    def rotate(a):
        other = jnp.where(front, pltpu.roll(a, PAD - HEAD // 2, 1), pltpu.roll(a, HEAD // 2, 1))
        return (a * cos + other * sin).astype(jnp.bfloat16)

    q, k = rotate(q), rotate(k)
    q_ref[...] = q[:TOK]
    k_ref[...] = k
    v_ref[...] = v
    attend(q[TOK:], k, v, mix_s, 0, TOK, same_place())
    give_ref[...] = regroup(mix_s[...], pltpu.roll)[:, :HALF].astype(jnp.bfloat16)


def temporal_own_kernel(q_ref, k_ref, v_ref, keep_ref, mix_s):
    attend(q_ref[...], k_ref[...], v_ref[...], mix_s, 0, TOK, same_place())
    keep_ref[...] = regroup(mix_s[...], pltpu.roll)[:, :HALF].astype(jnp.bfloat16)


def result_kernel(x_ref, own_ref, got_ref, rows_ref, gate_ref, w_ref, out_ref):
    added = mixed_dot(x_ref[0], own_ref[...], got_ref[...], w_ref, D, D)
    out_ref[...] = (rows_ref[...].astype(jnp.float32) + gate_ref[...] * added).astype(jnp.bfloat16)


VMEM_LIMIT = 32 * 2**20
VMEM = pl.BlockSpec(memory_space=pltpu.VMEM)
SMEM = pl.BlockSpec(memory_space=pltpu.SMEM)


def b16(*shape):
    return jax.ShapeDtypeStruct(shape, jnp.bfloat16)


def run(kernel, outs, specs, scratch, name, *operands):
    return pl.pallas_call(
        kernel,
        out_shape=outs,
        in_specs=specs,
        out_specs=jax.tree.map(lambda _: VMEM, outs),
        scratch_shapes=scratch,
        compiler_params=pltpu.CompilerParams(vmem_limit_bytes=VMEM_LIMIT),
        name=name,
    )(*operands)


def on_device(tokens, anchor, positions, w_spatial, w_temporal, mod_shift, mod_scale, mod_gate):
    index = lax.axis_index("frame")
    z, x, core = index // 4, index // 2 % 2, index % 2
    root = anchor[0]
    root_z, root_x, root_core = root // 4, root // 2 % 2, root % 2

    x_arg = jnp.reshape(x, (1,)).astype(jnp.int32)

    own = tokens[0]
    candidate = jnp.where(root_core == core, own, swap(own, CORE))
    mine = lax.dynamic_slice_in_dim(candidate, (2 * x + core) * 32, 32, 0)
    theirs = lax.dynamic_slice_in_dim(candidate, (2 * (1 - x) + core) * 32, 32, 0)
    theirs, own = lax.optimization_barrier((swap(theirs, X_LO), own))
    quarter = jnp.where(root_x == x, mine, theirs)
    side = jnp.where(z % 2 == 0, 1, -1)
    s_own = ring_gather(spatial_slabs(w_spatial, quarter, x), z, side)
    s_other = [swap(full, CORE) for full in s_own]

    pair = ordered(x, own, swap(own, X_LO), 0)
    normed = regroup(modulated_norm(pair, mod_shift[0], mod_scale[0]), jnp.roll)
    tokens_half = halves(pair, x)[0]
    gate_half = halves(mod_gate[:1], x)[0]
    t_slab = temporal_slab(w_temporal, x)

    w_qk, w_vo = [both_cores(s_own[i], s_other[i], core) for i in range(2)]
    t_slab, w_qk, w_vo = lax.optimization_barrier((t_slab, w_qk, w_vo))
    t_own = put(jnp.zeros((8,) + t_slab.shape, t_slab.dtype), t_slab, z)
    even, odd = swap(t_slab, Z_EVEN), swap(t_slab, Z_ODD)

    def chosen(full):
        return lax.dynamic_slice(full, (144 * root_z, D), (144, 256))

    near = quarter_rows(
        jnp.concatenate([chosen(w_qk), chosen(w_vo)], axis=1).reshape(2, 72, 512)
    )
    anchor_rows = jnp.concatenate([near, swap(near, X_LO)], axis=0)
    qk, v = run(
        project_kernel, (b16(2 * TOK, D), b16(2 * TOK, PAD)), [VMEM] * 3, [], "project",
        normed, w_qk, w_vo,
    )
    mix = run(
        spatial_kernel,
        b16(2 * TOK, HALF),
        [VMEM] * 7,
        [pltpu.VMEM((2 * TOK, PAD), jnp.float32)],
        "spatial",
        qk,
        v,
        anchor_rows,
        mod_shift[:1],
        mod_scale[:1],
        w_qk,
        w_vo,
    )

    def round_with(step, work, even, odd, t_own):
        work, even, odd = lax.optimization_barrier((work, even, odd))
        t_own = put(put(t_own, even, z + side * step), odd, z - side * step)
        return work, swap(odd, Z_EVEN), swap(even, Z_ODD), t_own

    mix, even, odd, t_own = round_with(1, mix, even, odd, t_own)
    hidden = run(
        hidden_kernel,
        b16(TOK, D),
        [SMEM] + [VMEM] * 5,
        [],
        "hidden",
        x_arg,
        mix,
        swap(mix, X_LO),
        tokens_half,
        gate_half,
        w_vo,
    )

    hidden, even, odd, t_own = round_with(2, hidden, even, odd, t_own)
    moved = lax.all_to_all(
        hidden.reshape(16, 8, D),
        "frame",
        split_axis=0,
        concat_axis=0,
        axis_index_groups=SAME_X,
        tiled=True,
    ).reshape(TOK, D)
    moved, even, odd = lax.optimization_barrier((moved, even, odd))
    t_own = put(put(t_own, even, z + side * 3), odd, z - side * 3)
    there = swap(moved, X_LO)
    cut = 1408
    last = jnp.concatenate([swap(odd[:, :cut], Z_EVEN), swap(even[:, cut:], Z_ODD)], axis=1)
    t_other = swap(t_own, CORE)
    t_w = both_cores(put(t_own, last, z + 4), put(t_other, swap(last, CORE), z + 4), core)

    half_size = HEAD // 2
    freqs = 10000.0 ** (-jnp.arange(half_size, dtype=jnp.float32) / half_size)
    by_x = positions.reshape(8, 2, 2).transpose(1, 0, 2)
    by_row = jnp.where(x == 0, by_x, by_x[::-1]).reshape(32)
    angles = by_row.astype(jnp.float32)[:, None] * freqs[None, :]
    cosine, sine = jnp.cos(angles), jnp.sin(angles)

    def spread(first, second):
        table = jnp.tile(jnp.concatenate([first, second], axis=1), (1, HEADS // 2))
        table = jnp.pad(table, ((0, 0), (0, PAD - HALF)))
        return jnp.broadcast_to(table[:, None], (32, 8, PAD)).reshape(2 * TOK, PAD)

    rows, t_normed = run(
        rows_kernel,
        (b16(TOK, D), b16(2 * TOK, D)),
        [SMEM] + [VMEM] * 4,
        [],
        "rows",
        x_arg,
        moved,
        there,
        mod_shift[1:],
        mod_scale[1:],
    )
    give, t_q, t_k, t_v = run(
        temporal_kernel,
        (b16(TOK, HALF), b16(TOK, PAD), b16(2 * TOK, PAD), b16(2 * TOK, PAD)),
        [VMEM] * 4,
        [pltpu.VMEM((TOK, PAD), jnp.float32)],
        "temporal",
        t_normed,
        spread(cosine, cosine),
        spread(-sine, sine),
        t_w,
    )
    keep = run(
        temporal_own_kernel,
        b16(TOK, HALF),
        [VMEM] * 3,
        [pltpu.VMEM((TOK, PAD), jnp.float32)],
        "temporal_own",
        t_q,
        t_k,
        t_v,
    )
    result = run(
        result_kernel,
        b16(TOK, D),
        [SMEM] + [VMEM] * 5,
        [],
        "result",
        x_arg,
        keep,
        swap(give, X_LO),
        rows,
        mod_gate[1:],
        t_w,
    )
    back = lax.all_to_all(
        result.reshape(16, 8, D),
        "frame",
        split_axis=0,
        concat_axis=0,
        axis_index_groups=SAME_X,
        tiled=True,
    )
    return back.reshape(1, TOK, D)


def solution(mesh):
    placed = (
        P(("batch", "frame"), None, None),
        P("batch"),
        P("batch"),
        P(None, "frame", None),
        P(None, "frame", None),
        P("batch", None),
        P("batch", None),
        P("batch", None),
    )
    return jax.shard_map(
        on_device,
        mesh=mesh,
        in_specs=placed,
        out_specs=P(("batch", "frame"), None, None),
        check_vma=False,
    )
```

```python
import math

import jax
import jax.numpy as jnp
from jax import lax
from jax.experimental import pallas as pl
from jax.experimental.pallas import tpu as pltpu
from jax.sharding import PartitionSpec as P

HEADS = 16
D = 1152
HALF = D // 2
HEAD = D // HEADS
PAD = 640
TOK = 128
FRAMES = 32
AXES = ("batch", "frame")
SAME_X = [[4 * z + 2 * x + core for z in range(8) for core in range(2)] for x in range(2)]


def build_perm(partner):
    pairs = []
    for x_hi in range(2):
        for y in range(4):
            for z in range(8):
                for x_lo in range(2):
                    for core in range(2):
                        x2, z2, c2 = partner(2 * x_hi + x_lo, z, core)
                        x2, z2 = x2 % 4, z2 % 8
                        source = (x_hi * 4 + y) * 32 + z * 4 + x_lo * 2 + core
                        target = ((x2 // 2) * 4 + y) * 32 + z2 * 4 + (x2 % 2) * 2 + c2
                        pairs.append((source, target))
    return pairs


CORE = build_perm(lambda x, z, c: (x, z, 1 - c))
X_LO = build_perm(lambda x, z, c: (x ^ 1, z, c))
X_CORE = build_perm(lambda x, z, c: (x ^ 1, z, 1 - c))
X_HI = build_perm(lambda x, z, c: (x + 1 if x % 2 else x - 1, z, c))
Z_EVEN = build_perm(lambda x, z, c: (x, z ^ 1, c))
Z_ODD = build_perm(lambda x, z, c: (x, z + 1 if z % 2 else z - 1, c))


def swap(value, pairs):
    return lax.ppermute(value, AXES, pairs)


def after(value, other):
    return lax.optimization_barrier((value, other))[0]


def modulated_norm(inputs, shift_row, scale_row):
    values = inputs.astype(jnp.float32)
    row_mean = jnp.mean(values, axis=-1, keepdims=True)
    centered = values - row_mean
    variance = jnp.mean(centered * centered, axis=-1, keepdims=True)
    return (centered * lax.rsqrt(variance + 1e-06) * (1.0 + scale_row) + shift_row).astype(
        jnp.bfloat16
    )


def ordered(place, own, other, axis):
    return jnp.where(
        place == 0,
        jnp.concatenate([own, other], axis=axis),
        jnp.concatenate([other, own], axis=axis),
    )


def regroup(a, roll):
    width = a.shape[-1]
    spot = lax.broadcasted_iota(jnp.int32, a.shape, a.ndim - 1) % 144
    ahead = roll(a, width - 36, a.ndim - 1)
    behind = roll(a, 36, a.ndim - 1)
    return jnp.where(
        (spot >= 36) & (spot < 72), ahead, jnp.where((spot >= 72) & (spot < 108), behind, a)
    )


def halves(a, x):
    low, high = a[..., :HALF], a[..., HALF:]
    return jnp.where(x == 0, low, high), jnp.where(x == 0, high, low)


def swap_rows(weights, x):
    own, other = halves(weights, x)
    own = jnp.concatenate([own[i] for i in range(4)], axis=-1)
    other = jnp.concatenate([other[i] for i in range(4)], axis=-1)
    return own, swap(other, X_HI)


def spatial_slabs(own, got, quarter, x):
    rows = ordered(x, own, got, 0)
    extra = quarter.reshape(8, 4, 9, 128).transpose(0, 2, 1, 3).reshape(72, 512)
    return (
        jnp.concatenate([rows[:, :D], extra[:, :256]], axis=1),
        jnp.concatenate([rows[:, D:], extra[:, 256:]], axis=1),
    )


def put(full, block, z_at):
    return lax.dynamic_update_slice(full, block[None], (z_at % 8, 0, 0))


def both_cores(own, other, core):
    full = jnp.stack(
        [jnp.where(core == 0, own, other), jnp.where(core == 0, other, own)], axis=1
    )
    return full.reshape(D, own.shape[-1])


def ring_gather(slabs, z, side):
    full = [put(jnp.zeros((8,) + slab.shape, slab.dtype), slab, z) for slab in slabs]
    even, odd = list(slabs), list(slabs)
    for step in (1, 2, 3):
        for i in range(2):
            even[i], odd[i] = swap(odd[i], Z_EVEN), swap(even[i], Z_ODD)
            full[i] = put(put(full[i], even[i], z + side * step), odd[i], z - side * step)
    full[0] = put(full[0], swap(odd[0], Z_EVEN), z + 4)
    full[1] = put(full[1], swap(even[1], Z_ODD), z + 4)
    return full


def quarter_rows(extra):
    return extra.reshape(-1, 8, 9, 4, 128).transpose(0, 1, 3, 2, 4).reshape(-1, D)


def temporal_slab(weights, x, ready):
    own, other = halves(weights[:3], x)
    pad = jnp.zeros((36, PAD - HALF), weights.dtype)
    own = jnp.concatenate([own[0], own[1], weights[3], own[2], pad], axis=-1)
    other = jnp.concatenate([other[0], other[1], weights[3], other[2], pad], axis=-1)
    return ordered(x, own, swap(after(other, ready), X_HI), 0)


def head_window(head):
    first = head * HEAD
    begin = first // 128 * 128
    end = -(-(first + HEAD) // 128) * 128
    return first, begin, end


def attend(q, k, v, mix_ref, row0, rows, bias):
    for head in range(HEADS // 2):
        first, begin, end = head_window(head)
        lane = lax.broadcasted_iota(jnp.int32, (1, end - begin), 1) + begin
        inside = (lane >= first) & (lane < first + HEAD)
        qw = jnp.where(inside, q[:, begin:end], 0).astype(jnp.bfloat16)
        scores = lax.dot_general(
            qw,
            k[:, begin:end],
            (((1,), (1,)), ((), ())),
            preferred_element_type=jnp.float32,
        ) * (1.0 / math.sqrt(HEAD))
        if bias is not None:
            scores = jnp.where(bias, scores, -1e30)
        top = jnp.max(scores, axis=-1, keepdims=True)
        weight = jnp.exp(scores - top)
        total = jnp.sum(weight, axis=-1, keepdims=True)
        out = jnp.dot(
            weight.astype(jnp.bfloat16), v[:, begin:end], preferred_element_type=jnp.float32
        ) / total
        here = mix_ref[row0 : row0 + rows, begin:end]
        mix_ref[row0 : row0 + rows, begin:end] = jnp.where(inside, out, here)


def norm_regroup(values, shift, scale):
    centered = values - jnp.mean(values, axis=-1, keepdims=True)
    variance = jnp.mean(centered * centered, axis=-1, keepdims=True)
    normed = centered * lax.rsqrt(variance + 1e-06) * (1.0 + scale) + shift
    return regroup(normed, pltpu.roll).astype(jnp.bfloat16)


def project_kernel(normed_ref, wa_ref, wb_ref, qk_ref, v_ref):
    normed = normed_ref[...]
    qk = jnp.dot(normed, wa_ref[:, :D], preferred_element_type=jnp.float32)
    qk_ref[...] = qk.astype(jnp.bfloat16)
    v = jnp.dot(normed, wb_ref[:, :PAD], preferred_element_type=jnp.float32)
    v_ref[...] = v.astype(jnp.bfloat16)


def spatial_kernel(
    qk_ref, v_ref, anchor_ref, shift_ref, scale_ref, wa_ref, wb_ref, out_ref, mix_s
):
    anchor = norm_regroup(anchor_ref[...].astype(jnp.float32), shift_ref[...], scale_ref[...])
    anchor_k = jnp.dot(anchor, wa_ref[:, 512:D], preferred_element_type=jnp.float32)
    anchor_v = jnp.dot(anchor, wb_ref[:, :PAD], preferred_element_type=jnp.float32).astype(
        jnp.bfloat16
    )
    anchor_k = pltpu.roll(anchor_k, PAD - 64, 1).astype(jnp.bfloat16)
    own_k = pltpu.roll(qk_ref[:, 512:].astype(jnp.float32), PAD - 64, 1).astype(jnp.bfloat16)
    for frame in range(2):
        r0 = frame * TOK
        keys = jnp.concatenate([own_k[r0 : r0 + TOK], anchor_k], axis=0)
        vals = jnp.concatenate([v_ref[r0 : r0 + TOK], anchor_v], axis=0)
        attend(qk_ref[r0 : r0 + TOK, :PAD], keys, vals, mix_s, r0, TOK, None)
    out_ref[...] = regroup(mix_s[...], pltpu.roll)[:, :HALF].astype(jnp.bfloat16)


def mixed_dot(x, own, got, w_ref, column, width):
    def part(side, values):
        rows = pl.ds(pl.multiple_of(side * HALF, HALF), HALF)
        return jnp.dot(
            values, w_ref[rows, column : column + width], preferred_element_type=jnp.float32
        )

    return part(x, own) + part(1 - x, got)


def hidden_kernel(x_ref, own_ref, got_ref, tokens_ref, gate_ref, wb_ref, out_ref):
    added = mixed_dot(x_ref[0], own_ref[...], got_ref[...], wb_ref, 512, PAD)
    added = pltpu.roll(added, PAD - 64, 1)[:, :HALF]
    hidden = (tokens_ref[...].astype(jnp.float32) + gate_ref[...] * added).astype(jnp.bfloat16)
    out_ref[:, :HALF] = hidden[:TOK]
    out_ref[:, HALF:] = hidden[TOK:]


def rows_kernel(x_ref, moved_ref, there_ref, shift_ref, scale_ref, rows_ref, normed_ref):
    x = x_ref[0]
    moved, there = moved_ref[...], there_ref[...]
    low = jnp.where(x == 0, moved, there)
    high = jnp.where(x == 0, there, moved)
    first = jnp.concatenate([low[:, :HALF], high[:, :HALF]], axis=1)
    second = jnp.concatenate([low[:, HALF:], high[:, HALF:]], axis=1)
    own = jnp.where(x == 0, first, second)
    rows_ref[...] = own
    values = jnp.concatenate([own, jnp.where(x == 0, second, first)], axis=0)
    normed_ref[...] = norm_regroup(values.astype(jnp.float32), shift_ref[...], scale_ref[...])


def same_place():
    place_r = lax.broadcasted_iota(jnp.int32, (TOK, 2 * TOK), 0) % 8
    place_c = lax.broadcasted_iota(jnp.int32, (TOK, 2 * TOK), 1) % 8
    return place_r == place_c


def temporal_kernel(
    normed_ref, cos_ref, sin_ref, w_ref, give_ref, q_ref, k_ref, v_ref, mix_s
):
    rows = 2 * TOK
    normed = normed_ref[...]
    lane = lax.broadcasted_iota(jnp.int32, (rows, PAD), 1)
    front = lane % HEAD < HEAD // 2
    cos, sin = cos_ref[...], sin_ref[...]
    q = jnp.dot(normed, w_ref[:, :PAD], preferred_element_type=jnp.float32)
    k = jnp.dot(normed, w_ref[:, 512:D], preferred_element_type=jnp.float32)
    k = pltpu.roll(k, PAD - 64, 1)
    v = jnp.dot(normed, w_ref[:, 2 * D :], preferred_element_type=jnp.float32)
    v = v.astype(jnp.bfloat16)

    def rotate(a):
        other = jnp.where(front, pltpu.roll(a, PAD - HEAD // 2, 1), pltpu.roll(a, HEAD // 2, 1))
        return (a * cos + other * sin).astype(jnp.bfloat16)

    q, k = rotate(q), rotate(k)
    q_ref[...] = q[:TOK]
    k_ref[...] = k
    v_ref[...] = v
    attend(q[TOK:], k, v, mix_s, 0, TOK, same_place())
    give_ref[...] = regroup(mix_s[...], pltpu.roll)[:, :HALF].astype(jnp.bfloat16)


def temporal_own_kernel(q_ref, k_ref, v_ref, keep_ref, mix_s):
    attend(q_ref[...], k_ref[...], v_ref[...], mix_s, 0, TOK, same_place())
    keep_ref[...] = regroup(mix_s[...], pltpu.roll)[:, :HALF].astype(jnp.bfloat16)


def result_kernel(x_ref, own_ref, got_ref, rows_ref, gate_ref, w_ref, out_ref):
    added = mixed_dot(x_ref[0], own_ref[...], got_ref[...], w_ref, D, D)
    out_ref[...] = (rows_ref[...].astype(jnp.float32) + gate_ref[...] * added).astype(jnp.bfloat16)


VMEM_LIMIT = 32 * 2**20
VMEM = pl.BlockSpec(memory_space=pltpu.VMEM)
SMEM = pl.BlockSpec(memory_space=pltpu.SMEM)


def b16(*shape):
    return jax.ShapeDtypeStruct(shape, jnp.bfloat16)


def run(kernel, outs, specs, scratch, name, *operands):
    return pl.pallas_call(
        kernel,
        out_shape=outs,
        in_specs=specs,
        out_specs=jax.tree.map(lambda _: VMEM, outs),
        scratch_shapes=scratch,
        compiler_params=pltpu.CompilerParams(vmem_limit_bytes=VMEM_LIMIT),
        name=name,
    )(*operands)


def on_device(tokens, anchor, positions, w_spatial, w_temporal, mod_shift, mod_scale, mod_gate):
    index = lax.axis_index("frame")
    z, x, core = index // 4, index // 2 % 2, index % 2
    root = anchor[0]
    root_z, root_x, root_core = root // 4, root // 2 % 2, root % 2

    x_arg = jnp.reshape(x, (1,)).astype(jnp.int32)

    own = tokens[0]
    s_rows, s_got = swap_rows(w_spatial, x)

    def rows_for(x_at, core_at):
        return lax.dynamic_slice_in_dim(own, (2 * x_at + core_at) * 32, 32, 0)

    quarter = jnp.where(
        root_x == x,
        jnp.where(root_core == core, rows_for(x, core), swap(rows_for(x, 1 - core), CORE)),
        jnp.where(
            root_core == core,
            swap(rows_for(1 - x, core), X_LO),
            swap(rows_for(1 - x, 1 - core), X_CORE),
        ),
    )
    side = jnp.where(z % 2 == 0, 1, -1)
    t_slab = temporal_slab(w_temporal, x, s_got)
    s_own = ring_gather(spatial_slabs(s_rows, s_got, quarter, x), z, side)
    s_other = [swap(full, CORE) for full in s_own]
    own = after(own, quarter)

    def chosen(full):
        return lax.dynamic_slice(full, (root_z, 0, D), (1, 72, 256))[0]

    near = quarter_rows(jnp.concatenate([chosen(s_own[0]), chosen(s_own[1])], axis=1))
    pairs = jnp.concatenate([near, swap(near, X_LO)], axis=0)
    anchor_rows = jnp.concatenate([pairs, swap(pairs, CORE)], axis=0)

    pair = ordered(x, own, swap(own, X_LO), 0)
    normed = regroup(modulated_norm(pair, mod_shift[0], mod_scale[0]), jnp.roll)
    tokens_half = halves(pair, x)[0]
    gate_half = halves(mod_gate[:1], x)[0]

    w_qk, w_vo = [both_cores(s_own[i], s_other[i], core) for i in range(2)]
    t_slab = after(t_slab, near)
    t_own = put(jnp.zeros((8,) + t_slab.shape, t_slab.dtype), t_slab, z)
    even, odd = swap(t_slab, Z_EVEN), swap(t_slab, Z_ODD)

    qk, v = run(
        project_kernel, (b16(2 * TOK, D), b16(2 * TOK, PAD)), [VMEM] * 3, [], "project",
        normed, w_qk, w_vo,
    )
    mix = run(
        spatial_kernel,
        b16(2 * TOK, HALF),
        [VMEM] * 7,
        [pltpu.VMEM((2 * TOK, PAD), jnp.float32)],
        "spatial",
        qk,
        v,
        anchor_rows,
        mod_shift[:1],
        mod_scale[:1],
        w_qk,
        w_vo,
    )

    def round_with(step, work, even, odd, t_own):
        work, even, odd = lax.optimization_barrier((work, even, odd))
        t_own = put(put(t_own, even, z + side * step), odd, z - side * step)
        return work, swap(odd, Z_EVEN), swap(even, Z_ODD), t_own

    mix, even, odd, t_own = round_with(1, mix, even, odd, t_own)
    hidden = run(
        hidden_kernel,
        b16(TOK, D),
        [SMEM] + [VMEM] * 5,
        [],
        "hidden",
        x_arg,
        mix,
        swap(mix, X_LO),
        tokens_half,
        gate_half,
        w_vo,
    )

    hidden, even, odd, t_own = round_with(2, hidden, even, odd, t_own)
    moved = lax.all_to_all(
        hidden.reshape(16, 8, D),
        "frame",
        split_axis=0,
        concat_axis=0,
        axis_index_groups=SAME_X,
        tiled=True,
    ).reshape(TOK, D)
    moved, even, odd = lax.optimization_barrier((moved, even, odd))
    t_own = put(put(t_own, even, z + side * 3), odd, z - side * 3)
    there = swap(moved, X_LO)
    cut = 1408
    last = jnp.concatenate([swap(odd[:, :cut], Z_EVEN), swap(even[:, cut:], Z_ODD)], axis=1)
    t_other = swap(t_own, CORE)
    t_w = both_cores(put(t_own, last, z + 4), put(t_other, swap(last, CORE), z + 4), core)

    half_size = HEAD // 2
    freqs = 10000.0 ** (-jnp.arange(half_size, dtype=jnp.float32) / half_size)
    by_x = positions.reshape(8, 2, 2).transpose(1, 0, 2)
    by_row = jnp.where(x == 0, by_x, by_x[::-1]).reshape(32)
    angles = by_row.astype(jnp.float32)[:, None] * freqs[None, :]
    cosine, sine = jnp.cos(angles), jnp.sin(angles)

    def spread(first, second):
        table = jnp.tile(jnp.concatenate([first, second], axis=1), (1, HEADS // 2))
        table = jnp.pad(table, ((0, 0), (0, PAD - HALF)))
        return jnp.broadcast_to(table[:, None], (32, 8, PAD)).reshape(2 * TOK, PAD)

    rows, t_normed = run(
        rows_kernel,
        (b16(TOK, D), b16(2 * TOK, D)),
        [SMEM] + [VMEM] * 4,
        [],
        "rows",
        x_arg,
        moved,
        there,
        mod_shift[1:],
        mod_scale[1:],
    )
    give, t_q, t_k, t_v = run(
        temporal_kernel,
        (b16(TOK, HALF), b16(TOK, PAD), b16(2 * TOK, PAD), b16(2 * TOK, PAD)),
        [VMEM] * 4,
        [pltpu.VMEM((TOK, PAD), jnp.float32)],
        "temporal",
        t_normed,
        spread(cosine, cosine),
        spread(-sine, sine),
        t_w,
    )
    keep = run(
        temporal_own_kernel,
        b16(TOK, HALF),
        [VMEM] * 3,
        [pltpu.VMEM((TOK, PAD), jnp.float32)],
        "temporal_own",
        t_q,
        t_k,
        t_v,
    )
    result = run(
        result_kernel,
        b16(TOK, D),
        [SMEM] + [VMEM] * 5,
        [],
        "result",
        x_arg,
        keep,
        swap(give, X_LO),
        rows,
        mod_gate[1:],
        t_w,
    )
    back = lax.all_to_all(
        result.reshape(16, 8, D),
        "frame",
        split_axis=0,
        concat_axis=0,
        axis_index_groups=SAME_X,
        tiled=True,
    )
    return back.reshape(1, TOK, D)


def solution(mesh):
    placed = (
        P(("batch", "frame"), None, None),
        P("batch"),
        P("batch"),
        P(None, "frame", None),
        P(None, "frame", None),
        P("batch", None),
        P("batch", None),
        P("batch", None),
    )
    return jax.shard_map(
        on_device,
        mesh=mesh,
        in_specs=placed,
        out_specs=P(("batch", "frame"), None, None),
        check_vma=False,
    )
```

```python
import math

import jax
import jax.numpy as jnp
from jax import lax
from jax.experimental import pallas as pl
from jax.experimental.pallas import tpu as pltpu
from jax.sharding import PartitionSpec as P

HEADS = 16
D = 1152
HALF = D // 2
HEAD = D // HEADS
PAD = 640
TOK = 128
FRAMES = 32
AXES = ("batch", "frame")
SAME_X = [[4 * z + 2 * x + core for z in range(8) for core in range(2)] for x in range(2)]


def build_perm(partner):
    pairs = []
    for x_hi in range(2):
        for y in range(4):
            for z in range(8):
                for x_lo in range(2):
                    for core in range(2):
                        x2, z2, c2 = partner(2 * x_hi + x_lo, z, core)
                        x2, z2 = x2 % 4, z2 % 8
                        source = (x_hi * 4 + y) * 32 + z * 4 + x_lo * 2 + core
                        target = ((x2 // 2) * 4 + y) * 32 + z2 * 4 + (x2 % 2) * 2 + c2
                        pairs.append((source, target))
    return pairs


CORE = build_perm(lambda x, z, c: (x, z, 1 - c))
X_LO = build_perm(lambda x, z, c: (x ^ 1, z, c))
X_CORE = build_perm(lambda x, z, c: (x ^ 1, z, 1 - c))
X_HI = build_perm(lambda x, z, c: (x + 1 if x % 2 else x - 1, z, c))
Z_EVEN = build_perm(lambda x, z, c: (x, z ^ 1, c))
Z_ODD = build_perm(lambda x, z, c: (x, z + 1 if z % 2 else z - 1, c))


def swap(value, pairs):
    return lax.ppermute(value, AXES, pairs)


def after(value, other):
    return lax.optimization_barrier((value, other))[0]


def modulated_norm(inputs, shift_row, scale_row):
    values = inputs.astype(jnp.float32)
    row_mean = jnp.mean(values, axis=-1, keepdims=True)
    centered = values - row_mean
    variance = jnp.mean(centered * centered, axis=-1, keepdims=True)
    return (centered * lax.rsqrt(variance + 1e-06) * (1.0 + scale_row) + shift_row).astype(
        jnp.bfloat16
    )


def ordered(place, own, other, axis):
    return jnp.where(
        place == 0,
        jnp.concatenate([own, other], axis=axis),
        jnp.concatenate([other, own], axis=axis),
    )


def regroup(a, roll):
    width = a.shape[-1]
    spot = lax.broadcasted_iota(jnp.int32, a.shape, a.ndim - 1) % 144
    ahead = roll(a, width - 36, a.ndim - 1)
    behind = roll(a, 36, a.ndim - 1)
    return jnp.where(
        (spot >= 36) & (spot < 72), ahead, jnp.where((spot >= 72) & (spot < 108), behind, a)
    )


def halves(a, x):
    low, high = a[..., :HALF], a[..., HALF:]
    return jnp.where(x == 0, low, high), jnp.where(x == 0, high, low)


def swap_rows(weights, x):
    own, other = halves(weights, x)
    own = jnp.concatenate([own[i] for i in range(4)], axis=-1)
    other = jnp.concatenate([other[i] for i in range(4)], axis=-1)
    return own, swap(other, X_HI)


def spatial_slabs(own, got, quarter, x):
    rows = ordered(x, own, got, 0)
    extra = quarter.reshape(4, 8, 9, 128).transpose(2, 1, 0, 3).reshape(72, 512)
    return (
        jnp.concatenate([rows[:, :D], extra[:, :256]], axis=1),
        jnp.concatenate([rows[:, D:], extra[:, 256:]], axis=1),
    )


def put(full, block, z_at):
    return lax.dynamic_update_slice(full, block[None], (z_at % 8, 0, 0))


def both_cores(own, other, core):
    full = jnp.stack(
        [jnp.where(core == 0, own, other), jnp.where(core == 0, other, own)], axis=1
    )
    return full.reshape(D, own.shape[-1])


def ring_gather(slabs, z, side):
    full = [put(jnp.zeros((8,) + slab.shape, slab.dtype), slab, z) for slab in slabs]
    even, odd = list(slabs), list(slabs)
    for step in (1, 2, 3):
        for i in range(2):
            even[i], odd[i] = swap(odd[i], Z_EVEN), swap(even[i], Z_ODD)
            full[i] = put(put(full[i], even[i], z + side * step), odd[i], z - side * step)
    full[0] = put(full[0], swap(odd[0], Z_EVEN), z + 4)
    full[1] = put(full[1], swap(even[1], Z_ODD), z + 4)
    return full


def quarter_rows(packed):
    return [
        jnp.concatenate(
            [packed[8 * c : 8 * c + 8, 128 * b : 128 * b + 128] for c in range(9)], axis=1
        )
        for b in range(4)
    ]


def temporal_slab(weights, x, ready):
    own, other = halves(weights[:3], x)
    pad = jnp.zeros((36, PAD - HALF), weights.dtype)
    own = jnp.concatenate([own[0], own[1], weights[3], own[2], pad], axis=-1)
    other = jnp.concatenate([other[0], other[1], weights[3], other[2], pad], axis=-1)
    return ordered(x, own, swap(after(other, ready), X_HI), 0)


def head_window(head):
    first = head * HEAD
    begin = first // 128 * 128
    end = -(-(first + HEAD) // 128) * 128
    return first, begin, end


def attend(q, k, v, mix_ref, row0, rows, bias):
    for head in range(HEADS // 2):
        first, begin, end = head_window(head)
        lane = lax.broadcasted_iota(jnp.int32, (1, end - begin), 1) + begin
        inside = (lane >= first) & (lane < first + HEAD)
        qw = jnp.where(inside, q[:, begin:end], 0).astype(jnp.bfloat16)
        scores = lax.dot_general(
            qw,
            k[:, begin:end],
            (((1,), (1,)), ((), ())),
            preferred_element_type=jnp.float32,
        ) * (1.0 / math.sqrt(HEAD))
        if bias is not None:
            scores = jnp.where(bias, scores, -1e30)
        top = jnp.max(scores, axis=-1, keepdims=True)
        weight = jnp.exp(scores - top)
        total = jnp.sum(weight, axis=-1, keepdims=True)
        out = jnp.dot(
            weight.astype(jnp.bfloat16), v[:, begin:end], preferred_element_type=jnp.float32
        ) / total
        here = mix_ref[row0 : row0 + rows, begin:end]
        mix_ref[row0 : row0 + rows, begin:end] = jnp.where(inside, out, here)


def norm_regroup(values, shift, scale):
    centered = values - jnp.mean(values, axis=-1, keepdims=True)
    variance = jnp.mean(centered * centered, axis=-1, keepdims=True)
    normed = centered * lax.rsqrt(variance + 1e-06) * (1.0 + scale) + shift
    return regroup(normed, pltpu.roll).astype(jnp.bfloat16)


def project_kernel(normed_ref, wa_ref, wb_ref, qk_ref, v_ref):
    normed = normed_ref[...]
    qk = jnp.dot(normed, wa_ref[:, :D], preferred_element_type=jnp.float32)
    qk_ref[...] = qk.astype(jnp.bfloat16)
    v = jnp.dot(normed, wb_ref[:, :PAD], preferred_element_type=jnp.float32)
    v_ref[...] = v.astype(jnp.bfloat16)


def spatial_kernel(
    qk_ref, v_ref, anchor_ref, shift_ref, scale_ref, wa_ref, wb_ref, out_ref, mix_s
):
    packed = anchor_ref[...].astype(jnp.float32)
    rows = [row for i in range(4) for row in quarter_rows(packed[72 * i : 72 * i + 72])]
    anchor = norm_regroup(jnp.concatenate(rows, axis=0), shift_ref[...], scale_ref[...])
    anchor_k = jnp.dot(anchor, wa_ref[:, 512:D], preferred_element_type=jnp.float32)
    anchor_v = jnp.dot(anchor, wb_ref[:, :PAD], preferred_element_type=jnp.float32).astype(
        jnp.bfloat16
    )
    anchor_k = pltpu.roll(anchor_k, PAD - 64, 1).astype(jnp.bfloat16)
    own_k = pltpu.roll(qk_ref[:, 512:].astype(jnp.float32), PAD - 64, 1).astype(jnp.bfloat16)
    for frame in range(2):
        r0 = frame * TOK
        keys = jnp.concatenate([own_k[r0 : r0 + TOK], anchor_k], axis=0)
        vals = jnp.concatenate([v_ref[r0 : r0 + TOK], anchor_v], axis=0)
        attend(qk_ref[r0 : r0 + TOK, :PAD], keys, vals, mix_s, r0, TOK, None)
    out_ref[...] = regroup(mix_s[...], pltpu.roll)[:, :HALF].astype(jnp.bfloat16)


def mixed_dot(x, own, got, w_ref, column, width):
    def part(side, values):
        rows = pl.ds(pl.multiple_of(side * HALF, HALF), HALF)
        return jnp.dot(
            values, w_ref[rows, column : column + width], preferred_element_type=jnp.float32
        )

    return part(x, own) + part(1 - x, got)


def hidden_kernel(x_ref, own_ref, got_ref, tokens_ref, gate_ref, wb_ref, out_ref):
    added = mixed_dot(x_ref[0], own_ref[...], got_ref[...], wb_ref, 512, PAD)
    added = pltpu.roll(added, PAD - 64, 1)[:, :HALF]
    hidden = (tokens_ref[...].astype(jnp.float32) + gate_ref[...] * added).astype(jnp.bfloat16)
    out_ref[:, :HALF] = hidden[:TOK]
    out_ref[:, HALF:] = hidden[TOK:]


def rows_kernel(x_ref, moved_ref, there_ref, shift_ref, scale_ref, rows_ref, normed_ref):
    x = x_ref[0]
    moved, there = moved_ref[...], there_ref[...]
    low = jnp.where(x == 0, moved, there)
    high = jnp.where(x == 0, there, moved)
    first = jnp.concatenate([low[:, :HALF], high[:, :HALF]], axis=1)
    second = jnp.concatenate([low[:, HALF:], high[:, HALF:]], axis=1)
    own = jnp.where(x == 0, first, second)
    rows_ref[...] = own
    values = jnp.concatenate([own, jnp.where(x == 0, second, first)], axis=0)
    normed_ref[...] = norm_regroup(values.astype(jnp.float32), shift_ref[...], scale_ref[...])


def same_place():
    place_r = lax.broadcasted_iota(jnp.int32, (TOK, 2 * TOK), 0) % 8
    place_c = lax.broadcasted_iota(jnp.int32, (TOK, 2 * TOK), 1) % 8
    return place_r == place_c


def temporal_kernel(
    normed_ref, cos_ref, sin_ref, w_ref, give_ref, q_ref, k_ref, v_ref, mix_s
):
    rows = 2 * TOK
    normed = normed_ref[...]
    lane = lax.broadcasted_iota(jnp.int32, (rows, PAD), 1)
    front = lane % HEAD < HEAD // 2
    cos, sin = cos_ref[...], sin_ref[...]
    q = jnp.dot(normed, w_ref[:, :PAD], preferred_element_type=jnp.float32)
    k = jnp.dot(normed, w_ref[:, 512:D], preferred_element_type=jnp.float32)
    k = pltpu.roll(k, PAD - 64, 1)
    v = jnp.dot(normed, w_ref[:, 2 * D :], preferred_element_type=jnp.float32)
    v = v.astype(jnp.bfloat16)

    def rotate(a):
        other = jnp.where(front, pltpu.roll(a, PAD - HEAD // 2, 1), pltpu.roll(a, HEAD // 2, 1))
        return (a * cos + other * sin).astype(jnp.bfloat16)

    q, k = rotate(q), rotate(k)
    q_ref[...] = q[:TOK]
    k_ref[...] = k
    v_ref[...] = v
    attend(q[TOK:], k, v, mix_s, 0, TOK, same_place())
    give_ref[...] = regroup(mix_s[...], pltpu.roll)[:, :HALF].astype(jnp.bfloat16)


def temporal_own_kernel(q_ref, k_ref, v_ref, keep_ref, mix_s):
    attend(q_ref[...], k_ref[...], v_ref[...], mix_s, 0, TOK, same_place())
    keep_ref[...] = regroup(mix_s[...], pltpu.roll)[:, :HALF].astype(jnp.bfloat16)


def result_kernel(x_ref, own_ref, got_ref, rows_ref, gate_ref, w_ref, out_ref):
    added = mixed_dot(x_ref[0], own_ref[...], got_ref[...], w_ref, D, D)
    out_ref[...] = (rows_ref[...].astype(jnp.float32) + gate_ref[...] * added).astype(jnp.bfloat16)


VMEM_LIMIT = 32 * 2**20
VMEM = pl.BlockSpec(memory_space=pltpu.VMEM)
SMEM = pl.BlockSpec(memory_space=pltpu.SMEM)


def b16(*shape):
    return jax.ShapeDtypeStruct(shape, jnp.bfloat16)


def run(kernel, outs, specs, scratch, name, *operands):
    return pl.pallas_call(
        kernel,
        out_shape=outs,
        in_specs=specs,
        out_specs=jax.tree.map(lambda _: VMEM, outs),
        scratch_shapes=scratch,
        compiler_params=pltpu.CompilerParams(vmem_limit_bytes=VMEM_LIMIT),
        name=name,
    )(*operands)


def on_device(tokens, anchor, positions, w_spatial, w_temporal, mod_shift, mod_scale, mod_gate):
    index = lax.axis_index("frame")
    z, x, core = index // 4, index // 2 % 2, index % 2
    root = anchor[0]
    root_z, root_x, root_core = root // 4, root // 2 % 2, root % 2

    x_arg = jnp.reshape(x, (1,)).astype(jnp.int32)

    own = tokens[0]
    s_rows, s_got = swap_rows(w_spatial, x)

    def rows_for(x_at, core_at):
        return lax.dynamic_slice_in_dim(own, (2 * x_at + core_at) * 32, 32, 0)

    quarter = jnp.where(
        root_x == x,
        jnp.where(root_core == core, rows_for(x, core), swap(rows_for(x, 1 - core), CORE)),
        jnp.where(
            root_core == core,
            swap(rows_for(1 - x, core), X_LO),
            swap(rows_for(1 - x, 1 - core), X_CORE),
        ),
    )
    side = jnp.where(z % 2 == 0, 1, -1)
    t_slab = temporal_slab(w_temporal, x, s_got)
    s_own = ring_gather(spatial_slabs(s_rows, s_got, quarter, x), z, side)
    s_other = [swap(full, CORE) for full in s_own]
    own = after(own, quarter)

    def chosen(full):
        return lax.dynamic_slice(full, (root_z, 0, D), (1, 72, 256))[0]

    near = jnp.concatenate([chosen(s_own[0]), chosen(s_own[1])], axis=1)
    pairs = jnp.concatenate([near, swap(near, X_LO)], axis=0)
    anchor_rows = jnp.concatenate([pairs, swap(pairs, CORE)], axis=0)

    pair = ordered(x, own, swap(own, X_LO), 0)
    normed = regroup(modulated_norm(pair, mod_shift[0], mod_scale[0]), jnp.roll)
    tokens_half = halves(pair, x)[0]
    gate_half = halves(mod_gate[:1], x)[0]

    w_qk, w_vo = [both_cores(s_own[i], s_other[i], core) for i in range(2)]
    t_slab = after(t_slab, near)
    t_own = put(jnp.zeros((8,) + t_slab.shape, t_slab.dtype), t_slab, z)
    even, odd = swap(t_slab, Z_EVEN), swap(t_slab, Z_ODD)

    qk, v = run(
        project_kernel, (b16(2 * TOK, D), b16(2 * TOK, PAD)), [VMEM] * 3, [], "project",
        normed, w_qk, w_vo,
    )
    mix = run(
        spatial_kernel,
        b16(2 * TOK, HALF),
        [VMEM] * 7,
        [pltpu.VMEM((2 * TOK, PAD), jnp.float32)],
        "spatial",
        qk,
        v,
        anchor_rows,
        mod_shift[:1],
        mod_scale[:1],
        w_qk,
        w_vo,
    )

    def round_with(step, work, even, odd, t_own):
        work, even, odd = lax.optimization_barrier((work, even, odd))
        t_own = put(put(t_own, even, z + side * step), odd, z - side * step)
        return work, swap(odd, Z_EVEN), swap(even, Z_ODD), t_own

    mix, even, odd, t_own = round_with(1, mix, even, odd, t_own)
    hidden = run(
        hidden_kernel,
        b16(TOK, D),
        [SMEM] + [VMEM] * 5,
        [],
        "hidden",
        x_arg,
        mix,
        swap(mix, X_LO),
        tokens_half,
        gate_half,
        w_vo,
    )

    hidden, even, odd, t_own = round_with(2, hidden, even, odd, t_own)
    moved = lax.all_to_all(
        hidden.reshape(16, 8, D),
        "frame",
        split_axis=0,
        concat_axis=0,
        axis_index_groups=SAME_X,
        tiled=True,
    ).reshape(TOK, D)
    moved, even, odd = lax.optimization_barrier((moved, even, odd))
    t_own = put(put(t_own, even, z + side * 3), odd, z - side * 3)
    there = swap(moved, X_LO)
    cut = 1408
    last = jnp.concatenate([swap(odd[:, :cut], Z_EVEN), swap(even[:, cut:], Z_ODD)], axis=1)
    t_other = swap(t_own, CORE)
    t_w = both_cores(put(t_own, last, z + 4), put(t_other, swap(last, CORE), z + 4), core)

    half_size = HEAD // 2
    freqs = 10000.0 ** (-jnp.arange(half_size, dtype=jnp.float32) / half_size)
    by_x = positions.reshape(8, 2, 2).transpose(1, 0, 2)
    by_row = jnp.where(x == 0, by_x, by_x[::-1]).reshape(32)
    angles = by_row.astype(jnp.float32)[:, None] * freqs[None, :]
    cosine, sine = jnp.cos(angles), jnp.sin(angles)

    def spread(first, second):
        table = jnp.tile(jnp.concatenate([first, second], axis=1), (1, HEADS // 2))
        table = jnp.pad(table, ((0, 0), (0, PAD - HALF)))
        return jnp.broadcast_to(table[:, None], (32, 8, PAD)).reshape(2 * TOK, PAD)

    rows, t_normed = run(
        rows_kernel,
        (b16(TOK, D), b16(2 * TOK, D)),
        [SMEM] + [VMEM] * 4,
        [],
        "rows",
        x_arg,
        moved,
        there,
        mod_shift[1:],
        mod_scale[1:],
    )
    give, t_q, t_k, t_v = run(
        temporal_kernel,
        (b16(TOK, HALF), b16(TOK, PAD), b16(2 * TOK, PAD), b16(2 * TOK, PAD)),
        [VMEM] * 4,
        [pltpu.VMEM((TOK, PAD), jnp.float32)],
        "temporal",
        t_normed,
        spread(cosine, cosine),
        spread(-sine, sine),
        t_w,
    )
    keep = run(
        temporal_own_kernel,
        b16(TOK, HALF),
        [VMEM] * 3,
        [pltpu.VMEM((TOK, PAD), jnp.float32)],
        "temporal_own",
        t_q,
        t_k,
        t_v,
    )
    result = run(
        result_kernel,
        b16(TOK, D),
        [SMEM] + [VMEM] * 5,
        [],
        "result",
        x_arg,
        keep,
        swap(give, X_LO),
        rows,
        mod_gate[1:],
        t_w,
    )
    back = lax.all_to_all(
        result.reshape(16, 8, D),
        "frame",
        split_axis=0,
        concat_axis=0,
        axis_index_groups=SAME_X,
        tiled=True,
    )
    return back.reshape(1, TOK, D)


def solution(mesh):
    placed = (
        P(("batch", "frame"), None, None),
        P("batch"),
        P("batch"),
        P(None, "frame", None),
        P(None, "frame", None),
        P("batch", None),
        P("batch", None),
        P("batch", None),
    )
    return jax.shard_map(
        on_device,
        mesh=mesh,
        in_specs=placed,
        out_specs=P(("batch", "frame"), None, None),
        check_vma=False,
    )
```

```python
import math

import jax
import jax.numpy as jnp
from jax import lax
from jax.experimental import pallas as pl
from jax.experimental.pallas import tpu as pltpu
from jax.sharding import PartitionSpec as P

HEADS = 16
D = 1152
HALF = D // 2
HEAD = D // HEADS
PAD = 640
TOK = 128
FRAMES = 32
AXES = ("batch", "frame")
SAME_X = [[4 * z + 2 * x + core for z in range(8) for core in range(2)] for x in range(2)]


def build_perm(partner):
    pairs = []
    for x_hi in range(2):
        for y in range(4):
            for z in range(8):
                for x_lo in range(2):
                    for core in range(2):
                        x2, z2, c2 = partner(2 * x_hi + x_lo, z, core)
                        x2, z2 = x2 % 4, z2 % 8
                        source = (x_hi * 4 + y) * 32 + z * 4 + x_lo * 2 + core
                        target = ((x2 // 2) * 4 + y) * 32 + z2 * 4 + (x2 % 2) * 2 + c2
                        pairs.append((source, target))
    return pairs


CORE = build_perm(lambda x, z, c: (x, z, 1 - c))
X_LO = build_perm(lambda x, z, c: (x ^ 1, z, c))
X_CORE = build_perm(lambda x, z, c: (x ^ 1, z, 1 - c))
X_HI = build_perm(lambda x, z, c: (x + 1 if x % 2 else x - 1, z, c))
Z_EVEN = build_perm(lambda x, z, c: (x, z ^ 1, c))
Z_ODD = build_perm(lambda x, z, c: (x, z + 1 if z % 2 else z - 1, c))


def swap(value, pairs):
    return lax.ppermute(value, AXES, pairs)


def after(value, other):
    return lax.optimization_barrier((value, other))[0]


def modulated_norm(inputs, shift_row, scale_row):
    values = inputs.astype(jnp.float32)
    row_mean = jnp.mean(values, axis=-1, keepdims=True)
    centered = values - row_mean
    variance = jnp.mean(centered * centered, axis=-1, keepdims=True)
    return (centered * lax.rsqrt(variance + 1e-06) * (1.0 + scale_row) + shift_row).astype(
        jnp.bfloat16
    )


def ordered(place, own, other, axis):
    return jnp.where(
        place == 0,
        jnp.concatenate([own, other], axis=axis),
        jnp.concatenate([other, own], axis=axis),
    )


def regroup(a, roll):
    width = a.shape[-1]
    spot = lax.broadcasted_iota(jnp.int32, a.shape, a.ndim - 1) % 144
    ahead = roll(a, width - 36, a.ndim - 1)
    behind = roll(a, 36, a.ndim - 1)
    return jnp.where(
        (spot >= 36) & (spot < 72), ahead, jnp.where((spot >= 72) & (spot < 108), behind, a)
    )


def halves(a, x):
    low, high = a[..., :HALF], a[..., HALF:]
    return jnp.where(x == 0, low, high), jnp.where(x == 0, high, low)


def swap_rows(weights, x):
    own, other = halves(weights, x)
    own = jnp.concatenate([own[i] for i in range(4)], axis=-1)
    other = jnp.concatenate([other[i] for i in range(4)], axis=-1)
    return own, swap(other, X_HI)


def spatial_slabs(own, got, quarter, x):
    rows = ordered(x, own, got, 0)
    extra = quarter.reshape(4, 8, 9, 128).transpose(2, 1, 0, 3).reshape(72, 512)
    return (
        jnp.concatenate([rows[:, :D], extra[:, :256]], axis=1),
        jnp.concatenate([rows[:, D:], extra[:, 256:]], axis=1),
    )


def put(full, block, z_at):
    return lax.dynamic_update_slice(full, block[None], (z_at % 8, 0, 0))


def both_cores(own, other, core):
    full = jnp.stack(
        [jnp.where(core == 0, own, other), jnp.where(core == 0, other, own)], axis=1
    )
    return full.reshape(D, own.shape[-1])


def ring_gather(slabs, z, side):
    full = [put(jnp.zeros((8,) + slab.shape, slab.dtype), slab, z) for slab in slabs]
    even, odd = list(slabs), list(slabs)
    for step in (1, 2, 3):
        for i in range(2):
            even[i], odd[i] = swap(odd[i], Z_EVEN), swap(even[i], Z_ODD)
            full[i] = put(put(full[i], even[i], z + side * step), odd[i], z - side * step)
    full[0] = put(full[0], swap(odd[0], Z_EVEN), z + 4)
    full[1] = put(full[1], swap(even[1], Z_ODD), z + 4)
    return full


def quarter_rows(packed):
    return [
        jnp.concatenate(
            [packed[8 * c : 8 * c + 8, 128 * b : 128 * b + 128] for c in range(9)], axis=1
        )
        for b in range(4)
    ]


def temporal_slab(weights, x, ready):
    own, other = halves(weights[:3], x)
    pad = jnp.zeros((36, PAD - HALF), weights.dtype)
    own = jnp.concatenate([own[0], own[1], weights[3], own[2], pad], axis=-1)
    other = jnp.concatenate([other[0], other[1], weights[3], other[2], pad], axis=-1)
    return ordered(x, own, swap(after(other, ready), X_HI), 0)


def head_window(head):
    first = head * HEAD
    begin = first // 128 * 128
    end = -(-(first + HEAD) // 128) * 128
    return first, begin, end


def attend(q, k, v, mix_ref, row0, rows, bias):
    tiles = [jnp.zeros((rows, 128), jnp.float32)] * (PAD // 128)
    for group in range(0, HEADS // 2, 4):
        windows, weights, shares = [], [], []
        for head in range(group, group + 4):
            first, begin, end = head_window(head)
            lane = lax.broadcasted_iota(jnp.int32, (1, end - begin), 1) + begin
            inside = (lane >= first) & (lane < first + HEAD)
            windows.append((begin, end, inside))
            qw = jnp.where(inside, q[:, begin:end], 0).astype(jnp.bfloat16)
            weights.append(
                lax.dot_general(
                    qw,
                    k[:, begin:end],
                    (((1,), (1,)), ((), ())),
                    preferred_element_type=jnp.float32,
                )
            )
        for i, scores in enumerate(weights):
            if bias is not None:
                scores = jnp.where(bias, scores, -1e30)
            top = jnp.max(scores, axis=-1, keepdims=True)
            weight = jnp.exp2((scores - top) * (math.log2(math.e) / math.sqrt(HEAD)))
            shares.append(1.0 / jnp.sum(weight, axis=-1, keepdims=True))
            weights[i] = weight.astype(jnp.bfloat16)
        for (begin, end, inside), weight, share in zip(windows, weights, shares):
            out = jnp.dot(weight, v[:, begin:end], preferred_element_type=jnp.float32) * share
            for lane in range(0, end - begin, 128):
                tile = (begin + lane) // 128
                tiles[tile] = jnp.where(
                    inside[:, lane : lane + 128], out[:, lane : lane + 128], tiles[tile]
                )
    for tile, values in enumerate(tiles):
        mix_ref[row0 : row0 + rows, 128 * tile : 128 * tile + 128] = values


def norm_regroup(values, shift, scale):
    centered = values - jnp.mean(values, axis=-1, keepdims=True)
    variance = jnp.mean(centered * centered, axis=-1, keepdims=True)
    normed = centered * lax.rsqrt(variance + 1e-06) * (1.0 + scale) + shift
    return regroup(normed, pltpu.roll).astype(jnp.bfloat16)


def project_kernel(normed_ref, wa_ref, wb_ref, qk_ref, v_ref):
    normed = normed_ref[...]
    qk = jnp.dot(normed, wa_ref[:, :D], preferred_element_type=jnp.float32)
    qk_ref[...] = qk.astype(jnp.bfloat16)
    v = jnp.dot(normed, wb_ref[:, :PAD], preferred_element_type=jnp.float32)
    v_ref[...] = v.astype(jnp.bfloat16)


def spatial_kernel(
    qk_ref, v_ref, anchor_ref, shift_ref, scale_ref, wa_ref, wb_ref, out_ref, mix_s
):
    packed = anchor_ref[...].astype(jnp.float32)
    rows = [row for i in range(4) for row in quarter_rows(packed[72 * i : 72 * i + 72])]
    anchor = norm_regroup(jnp.concatenate(rows, axis=0), shift_ref[...], scale_ref[...])
    anchor_k = jnp.dot(anchor, wa_ref[:, 512:D], preferred_element_type=jnp.float32)
    anchor_v = jnp.dot(anchor, wb_ref[:, :PAD], preferred_element_type=jnp.float32).astype(
        jnp.bfloat16
    )
    anchor_k = pltpu.roll(anchor_k, PAD - 64, 1).astype(jnp.bfloat16)
    own_k = pltpu.roll(qk_ref[:, 512:].astype(jnp.float32), PAD - 64, 1).astype(jnp.bfloat16)
    for frame in range(2):
        r0 = frame * TOK
        keys = jnp.concatenate([own_k[r0 : r0 + TOK], anchor_k], axis=0)
        vals = jnp.concatenate([v_ref[r0 : r0 + TOK], anchor_v], axis=0)
        attend(qk_ref[r0 : r0 + TOK, :PAD], keys, vals, mix_s, r0, TOK, None)
    out_ref[...] = regroup(mix_s[...], pltpu.roll)[:, :HALF].astype(jnp.bfloat16)


def mixed_dot(x, own, got, w_ref, column, width):
    def part(side, values):
        rows = pl.ds(pl.multiple_of(side * HALF, HALF), HALF)
        return jnp.dot(
            values, w_ref[rows, column : column + width], preferred_element_type=jnp.float32
        )

    return part(x, own) + part(1 - x, got)


def hidden_kernel(x_ref, own_ref, got_ref, tokens_ref, gate_ref, wb_ref, out_ref):
    added = mixed_dot(x_ref[0], own_ref[...], got_ref[...], wb_ref, 512, PAD)
    added = pltpu.roll(added, PAD - 64, 1)[:, :HALF]
    hidden = (tokens_ref[...].astype(jnp.float32) + gate_ref[...] * added).astype(jnp.bfloat16)
    out_ref[:, :HALF] = hidden[:TOK]
    out_ref[:, HALF:] = hidden[TOK:]


def rows_kernel(x_ref, moved_ref, there_ref, shift_ref, scale_ref, rows_ref, normed_ref):
    x = x_ref[0]
    moved, there = moved_ref[...], there_ref[...]
    low = jnp.where(x == 0, moved, there)
    high = jnp.where(x == 0, there, moved)
    first = jnp.concatenate([low[:, :HALF], high[:, :HALF]], axis=1)
    second = jnp.concatenate([low[:, HALF:], high[:, HALF:]], axis=1)
    own = jnp.where(x == 0, first, second)
    rows_ref[...] = own
    values = jnp.concatenate([own, jnp.where(x == 0, second, first)], axis=0)
    normed_ref[...] = norm_regroup(values.astype(jnp.float32), shift_ref[...], scale_ref[...])


def same_place():
    place_r = lax.broadcasted_iota(jnp.int32, (TOK, 2 * TOK), 0) % 8
    place_c = lax.broadcasted_iota(jnp.int32, (TOK, 2 * TOK), 1) % 8
    return place_r == place_c


def temporal_kernel(
    normed_ref, cos_ref, sin_ref, w_ref, give_ref, q_ref, k_ref, v_ref, mix_s
):
    rows = 2 * TOK
    normed = normed_ref[...]
    lane = lax.broadcasted_iota(jnp.int32, (rows, PAD), 1)
    front = lane % HEAD < HEAD // 2
    cos, sin = cos_ref[...], sin_ref[...]
    q = jnp.dot(normed, w_ref[:, :PAD], preferred_element_type=jnp.float32)
    k = jnp.dot(normed, w_ref[:, 512:D], preferred_element_type=jnp.float32)
    k = pltpu.roll(k, PAD - 64, 1)
    v = jnp.dot(normed, w_ref[:, 2 * D :], preferred_element_type=jnp.float32)
    v = v.astype(jnp.bfloat16)

    def rotate(a):
        other = jnp.where(front, pltpu.roll(a, PAD - HEAD // 2, 1), pltpu.roll(a, HEAD // 2, 1))
        return (a * cos + other * sin).astype(jnp.bfloat16)

    q, k = rotate(q), rotate(k)
    q_ref[...] = q[:TOK]
    k_ref[...] = k
    v_ref[...] = v
    attend(q[TOK:], k, v, mix_s, 0, TOK, same_place())
    give_ref[...] = regroup(mix_s[...], pltpu.roll)[:, :HALF].astype(jnp.bfloat16)


def temporal_own_kernel(q_ref, k_ref, v_ref, keep_ref, mix_s):
    attend(q_ref[...], k_ref[...], v_ref[...], mix_s, 0, TOK, same_place())
    keep_ref[...] = regroup(mix_s[...], pltpu.roll)[:, :HALF].astype(jnp.bfloat16)


def result_kernel(x_ref, own_ref, got_ref, rows_ref, gate_ref, w_ref, out_ref):
    added = mixed_dot(x_ref[0], own_ref[...], got_ref[...], w_ref, D, D)
    out_ref[...] = (rows_ref[...].astype(jnp.float32) + gate_ref[...] * added).astype(jnp.bfloat16)


VMEM_LIMIT = 32 * 2**20
VMEM = pl.BlockSpec(memory_space=pltpu.VMEM)
SMEM = pl.BlockSpec(memory_space=pltpu.SMEM)


def b16(*shape):
    return jax.ShapeDtypeStruct(shape, jnp.bfloat16)


def run(kernel, outs, specs, scratch, name, *operands):
    return pl.pallas_call(
        kernel,
        out_shape=outs,
        in_specs=specs,
        out_specs=jax.tree.map(lambda _: VMEM, outs),
        scratch_shapes=scratch,
        compiler_params=pltpu.CompilerParams(vmem_limit_bytes=VMEM_LIMIT),
        name=name,
    )(*operands)


def on_device(tokens, anchor, positions, w_spatial, w_temporal, mod_shift, mod_scale, mod_gate):
    index = lax.axis_index("frame")
    z, x, core = index // 4, index // 2 % 2, index % 2
    root = anchor[0]
    root_z, root_x, root_core = root // 4, root // 2 % 2, root % 2

    x_arg = jnp.reshape(x, (1,)).astype(jnp.int32)

    own = tokens[0]
    s_rows, s_got = swap_rows(w_spatial, x)

    def rows_for(x_at, core_at):
        return lax.dynamic_slice_in_dim(own, (2 * x_at + core_at) * 32, 32, 0)

    quarter = jnp.where(
        root_x == x,
        jnp.where(root_core == core, rows_for(x, core), swap(rows_for(x, 1 - core), CORE)),
        jnp.where(
            root_core == core,
            swap(rows_for(1 - x, core), X_LO),
            swap(rows_for(1 - x, 1 - core), X_CORE),
        ),
    )
    side = jnp.where(z % 2 == 0, 1, -1)
    t_slab = temporal_slab(w_temporal, x, s_got)
    s_own = ring_gather(spatial_slabs(s_rows, s_got, quarter, x), z, side)
    s_other = [swap(full, CORE) for full in s_own]
    own = after(own, quarter)

    def chosen(full):
        return lax.dynamic_slice(full, (root_z, 0, D), (1, 72, 256))[0]

    near = jnp.concatenate([chosen(s_own[0]), chosen(s_own[1])], axis=1)
    pairs = jnp.concatenate([near, swap(near, X_LO)], axis=0)
    anchor_rows = jnp.concatenate([pairs, swap(pairs, CORE)], axis=0)

    pair = ordered(x, own, swap(own, X_LO), 0)
    normed = regroup(modulated_norm(pair, mod_shift[0], mod_scale[0]), jnp.roll)
    tokens_half = halves(pair, x)[0]
    gate_half = halves(mod_gate[:1], x)[0]

    w_qk, w_vo = [both_cores(s_own[i], s_other[i], core) for i in range(2)]
    t_slab = after(t_slab, near)
    t_own = put(jnp.zeros((8,) + t_slab.shape, t_slab.dtype), t_slab, z)
    even, odd = swap(t_slab, Z_EVEN), swap(t_slab, Z_ODD)

    qk, v = run(
        project_kernel, (b16(2 * TOK, D), b16(2 * TOK, PAD)), [VMEM] * 3, [], "project",
        normed, w_qk, w_vo,
    )
    mix = run(
        spatial_kernel,
        b16(2 * TOK, HALF),
        [VMEM] * 7,
        [pltpu.VMEM((2 * TOK, PAD), jnp.float32)],
        "spatial",
        qk,
        v,
        anchor_rows,
        mod_shift[:1],
        mod_scale[:1],
        w_qk,
        w_vo,
    )

    def round_with(step, work, even, odd, t_own):
        work, even, odd = lax.optimization_barrier((work, even, odd))
        t_own = put(put(t_own, even, z + side * step), odd, z - side * step)
        return work, swap(odd, Z_EVEN), swap(even, Z_ODD), t_own

    mix, even, odd, t_own = round_with(1, mix, even, odd, t_own)
    hidden = run(
        hidden_kernel,
        b16(TOK, D),
        [SMEM] + [VMEM] * 5,
        [],
        "hidden",
        x_arg,
        mix,
        swap(mix, X_LO),
        tokens_half,
        gate_half,
        w_vo,
    )

    hidden, even, odd, t_own = round_with(2, hidden, even, odd, t_own)
    moved = lax.all_to_all(
        hidden.reshape(16, 8, D),
        "frame",
        split_axis=0,
        concat_axis=0,
        axis_index_groups=SAME_X,
        tiled=True,
    ).reshape(TOK, D)
    moved, even, odd = lax.optimization_barrier((moved, even, odd))
    t_own = put(put(t_own, even, z + side * 3), odd, z - side * 3)
    there = swap(moved, X_LO)
    cut = 1408
    last = jnp.concatenate([swap(odd[:, :cut], Z_EVEN), swap(even[:, cut:], Z_ODD)], axis=1)
    t_other = swap(t_own, CORE)
    t_w = both_cores(put(t_own, last, z + 4), put(t_other, swap(last, CORE), z + 4), core)

    half_size = HEAD // 2
    freqs = 10000.0 ** (-jnp.arange(half_size, dtype=jnp.float32) / half_size)
    by_x = positions.reshape(8, 2, 2).transpose(1, 0, 2)
    by_row = jnp.where(x == 0, by_x, by_x[::-1]).reshape(32)
    angles = by_row.astype(jnp.float32)[:, None] * freqs[None, :]
    cosine, sine = jnp.cos(angles), jnp.sin(angles)

    def spread(first, second):
        table = jnp.tile(jnp.concatenate([first, second], axis=1), (1, HEADS // 2))
        table = jnp.pad(table, ((0, 0), (0, PAD - HALF)))
        return jnp.broadcast_to(table[:, None], (32, 8, PAD)).reshape(2 * TOK, PAD)

    rows, t_normed = run(
        rows_kernel,
        (b16(TOK, D), b16(2 * TOK, D)),
        [SMEM] + [VMEM] * 4,
        [],
        "rows",
        x_arg,
        moved,
        there,
        mod_shift[1:],
        mod_scale[1:],
    )
    give, t_q, t_k, t_v = run(
        temporal_kernel,
        (b16(TOK, HALF), b16(TOK, PAD), b16(2 * TOK, PAD), b16(2 * TOK, PAD)),
        [VMEM] * 4,
        [pltpu.VMEM((TOK, PAD), jnp.float32)],
        "temporal",
        t_normed,
        spread(cosine, cosine),
        spread(-sine, sine),
        t_w,
    )
    keep = run(
        temporal_own_kernel,
        b16(TOK, HALF),
        [VMEM] * 3,
        [pltpu.VMEM((TOK, PAD), jnp.float32)],
        "temporal_own",
        t_q,
        t_k,
        t_v,
    )
    result = run(
        result_kernel,
        b16(TOK, D),
        [SMEM] + [VMEM] * 5,
        [],
        "result",
        x_arg,
        keep,
        swap(give, X_LO),
        rows,
        mod_gate[1:],
        t_w,
    )
    back = lax.all_to_all(
        result.reshape(16, 8, D),
        "frame",
        split_axis=0,
        concat_axis=0,
        axis_index_groups=SAME_X,
        tiled=True,
    )
    return back.reshape(1, TOK, D)


def solution(mesh):
    placed = (
        P(("batch", "frame"), None, None),
        P("batch"),
        P("batch"),
        P(None, "frame", None),
        P(None, "frame", None),
        P("batch", None),
        P("batch", None),
        P("batch", None),
    )
    return jax.shard_map(
        on_device,
        mesh=mesh,
        in_specs=placed,
        out_specs=P(("batch", "frame"), None, None),
        check_vma=False,
    )
```

```python
import math

import jax
import jax.numpy as jnp
from jax import lax
from jax.experimental import pallas as pl
from jax.experimental.pallas import tpu as pltpu
from jax.sharding import PartitionSpec as P

HEADS = 16
D = 1152
HALF = D // 2
HEAD = D // HEADS
PAD = 640
TOK = 128
FRAMES = 32
AXES = ("batch", "frame")
SAME_X = [[4 * z + 2 * x + core for z in range(8) for core in range(2)] for x in range(2)]


def build_perm(partner):
    pairs = []
    for x_hi in range(2):
        for y in range(4):
            for z in range(8):
                for x_lo in range(2):
                    for core in range(2):
                        x2, z2, c2 = partner(2 * x_hi + x_lo, z, core)
                        x2, z2 = x2 % 4, z2 % 8
                        source = (x_hi * 4 + y) * 32 + z * 4 + x_lo * 2 + core
                        target = ((x2 // 2) * 4 + y) * 32 + z2 * 4 + (x2 % 2) * 2 + c2
                        pairs.append((source, target))
    return pairs


CORE = build_perm(lambda x, z, c: (x, z, 1 - c))
X_LO = build_perm(lambda x, z, c: (x ^ 1, z, c))
X_CORE = build_perm(lambda x, z, c: (x ^ 1, z, 1 - c))
X_HI = build_perm(lambda x, z, c: (x + 1 if x % 2 else x - 1, z, c))
Z_EVEN = build_perm(lambda x, z, c: (x, z ^ 1, c))
Z_ODD = build_perm(lambda x, z, c: (x, z + 1 if z % 2 else z - 1, c))


def swap(value, pairs):
    return lax.ppermute(value, AXES, pairs)


def after(value, other):
    return lax.optimization_barrier((value, other))[0]


def modulated_norm(inputs, shift_row, scale_row):
    values = inputs.astype(jnp.float32)
    row_mean = jnp.mean(values, axis=-1, keepdims=True)
    centered = values - row_mean
    variance = jnp.mean(centered * centered, axis=-1, keepdims=True)
    return (centered * lax.rsqrt(variance + 1e-06) * (1.0 + scale_row) + shift_row).astype(
        jnp.bfloat16
    )


def ordered(place, own, other, axis):
    return jnp.where(
        place == 0,
        jnp.concatenate([own, other], axis=axis),
        jnp.concatenate([other, own], axis=axis),
    )


def regroup(a, roll):
    width = a.shape[-1]
    spot = lax.broadcasted_iota(jnp.int32, a.shape, a.ndim - 1) % 144
    ahead = roll(a, width - 36, a.ndim - 1)
    behind = roll(a, 36, a.ndim - 1)
    return jnp.where(
        (spot >= 36) & (spot < 72), ahead, jnp.where((spot >= 72) & (spot < 108), behind, a)
    )


def halves(a, x):
    low, high = a[..., :HALF], a[..., HALF:]
    return jnp.where(x == 0, low, high), jnp.where(x == 0, high, low)


def swap_rows(weights, x):
    own, other = halves(weights, x)
    own = jnp.concatenate([own[i] for i in range(4)], axis=-1)
    other = jnp.concatenate([other[i] for i in range(4)], axis=-1)
    return own, swap(other, X_HI)


def spatial_slabs(own, got, quarter, x):
    rows = ordered(x, own, got, 0)
    extra = quarter.reshape(4, 8, 9, 128).transpose(2, 1, 0, 3).reshape(72, 512)
    return (
        jnp.concatenate([rows[:, :D], extra[:, :256]], axis=1),
        jnp.concatenate([rows[:, D:], extra[:, 256:]], axis=1),
    )


def put(full, block, z_at):
    return lax.dynamic_update_slice(full, block[None], (z_at % 8, 0, 0))


def both_cores(own, other, core):
    full = jnp.stack(
        [jnp.where(core == 0, own, other), jnp.where(core == 0, other, own)], axis=1
    )
    return full.reshape(D, own.shape[-1])


def ring_gather(slabs, z, side):
    full = [put(jnp.zeros((8,) + slab.shape, slab.dtype), slab, z) for slab in slabs]
    even, odd = list(slabs), list(slabs)
    for step in (1, 2, 3):
        for i in range(2):
            even[i], odd[i] = swap(odd[i], Z_EVEN), swap(even[i], Z_ODD)
            full[i] = put(put(full[i], even[i], z + side * step), odd[i], z - side * step)
    full[0] = put(full[0], swap(odd[0], Z_EVEN), z + 4)
    full[1] = put(full[1], swap(even[1], Z_ODD), z + 4)
    return full


def quarter_rows(packed):
    return [
        jnp.concatenate(
            [packed[8 * c : 8 * c + 8, 128 * b : 128 * b + 128] for c in range(9)], axis=1
        )
        for b in range(4)
    ]


def temporal_slab(weights, x, ready):
    own, other = halves(weights[:3], x)
    pad = jnp.zeros((36, PAD - HALF), weights.dtype)
    own = jnp.concatenate([own[0], own[1], weights[3], own[2], pad], axis=-1)
    other = jnp.concatenate([other[0], other[1], weights[3], other[2], pad], axis=-1)
    return ordered(x, own, swap(after(other, ready), X_HI), 0)


def head_window(head):
    first = head * HEAD
    begin = first // 128 * 128
    end = -(-(first + HEAD) // 128) * 128
    return first, begin, end


def attend(q, k, v, mix_ref, row0, rows, bias):
    tiles = [jnp.zeros((rows, 128), jnp.float32)] * (PAD // 128)
    for group in range(0, HEADS // 2, 8):
        windows, weights, shares = [], [], []
        for head in range(group, group + 8):
            first, begin, end = head_window(head)
            lane = lax.broadcasted_iota(jnp.int32, (1, end - begin), 1) + begin
            inside = (lane >= first) & (lane < first + HEAD)
            windows.append((begin, end, inside))
            qw = jnp.where(inside, q[:, begin:end], 0).astype(jnp.bfloat16)
            weights.append(
                lax.dot_general(
                    qw,
                    k[:, begin:end],
                    (((1,), (1,)), ((), ())),
                    preferred_element_type=jnp.float32,
                )
            )
        for i, scores in enumerate(weights):
            if bias is not None:
                scores = jnp.where(bias, scores, -1e30)
            top = jnp.max(scores, axis=-1, keepdims=True)
            weight = jnp.exp2((scores - top) * (math.log2(math.e) / math.sqrt(HEAD)))
            shares.append(1.0 / jnp.sum(weight, axis=-1, keepdims=True))
            weights[i] = weight.astype(jnp.bfloat16)
        for (begin, end, inside), weight, share in zip(windows, weights, shares):
            out = jnp.dot(weight, v[:, begin:end], preferred_element_type=jnp.float32) * share
            for lane in range(0, end - begin, 128):
                tile = (begin + lane) // 128
                tiles[tile] = jnp.where(
                    inside[:, lane : lane + 128], out[:, lane : lane + 128], tiles[tile]
                )
    for tile, values in enumerate(tiles):
        mix_ref[row0 : row0 + rows, 128 * tile : 128 * tile + 128] = values


def norm_regroup(values, shift, scale):
    centered = values - jnp.mean(values, axis=-1, keepdims=True)
    variance = jnp.mean(centered * centered, axis=-1, keepdims=True)
    normed = centered * lax.rsqrt(variance + 1e-06) * (1.0 + scale) + shift
    return regroup(normed, pltpu.roll).astype(jnp.bfloat16)


def project_kernel(normed_ref, wa_ref, wb_ref, qk_ref, v_ref):
    normed = normed_ref[...]
    qk = jnp.dot(normed, wa_ref[:, :D], preferred_element_type=jnp.float32)
    qk_ref[...] = qk.astype(jnp.bfloat16)
    v = jnp.dot(normed, wb_ref[:, :PAD], preferred_element_type=jnp.float32)
    v_ref[...] = v.astype(jnp.bfloat16)


def spatial_kernel(
    qk_ref, v_ref, anchor_ref, shift_ref, scale_ref, wa_ref, wb_ref, out_ref, mix_s
):
    packed = anchor_ref[...].astype(jnp.float32)
    rows = [row for i in range(4) for row in quarter_rows(packed[72 * i : 72 * i + 72])]
    anchor = norm_regroup(jnp.concatenate(rows, axis=0), shift_ref[...], scale_ref[...])
    anchor_k = jnp.dot(anchor, wa_ref[:, 512:D], preferred_element_type=jnp.float32)
    anchor_v = jnp.dot(anchor, wb_ref[:, :PAD], preferred_element_type=jnp.float32).astype(
        jnp.bfloat16
    )
    anchor_k = pltpu.roll(anchor_k, PAD - 64, 1).astype(jnp.bfloat16)
    own_k = pltpu.roll(qk_ref[:, 512:].astype(jnp.float32), PAD - 64, 1).astype(jnp.bfloat16)
    for frame in range(2):
        r0 = frame * TOK
        keys = jnp.concatenate([own_k[r0 : r0 + TOK], anchor_k], axis=0)
        vals = jnp.concatenate([v_ref[r0 : r0 + TOK], anchor_v], axis=0)
        attend(qk_ref[r0 : r0 + TOK, :PAD], keys, vals, mix_s, r0, TOK, None)
    out_ref[...] = regroup(mix_s[...], pltpu.roll)[:, :HALF].astype(jnp.bfloat16)


def mixed_dot(x, own, got, w_ref, column, width):
    def part(side, values):
        rows = pl.ds(pl.multiple_of(side * HALF, HALF), HALF)
        return jnp.dot(
            values, w_ref[rows, column : column + width], preferred_element_type=jnp.float32
        )

    return part(x, own) + part(1 - x, got)


def hidden_kernel(x_ref, own_ref, got_ref, tokens_ref, gate_ref, wb_ref, out_ref):
    added = mixed_dot(x_ref[0], own_ref[...], got_ref[...], wb_ref, 512, PAD)
    added = pltpu.roll(added, PAD - 64, 1)[:, :HALF]
    hidden = (tokens_ref[...].astype(jnp.float32) + gate_ref[...] * added).astype(jnp.bfloat16)
    out_ref[:, :HALF] = hidden[:TOK]
    out_ref[:, HALF:] = hidden[TOK:]


def rows_kernel(x_ref, moved_ref, there_ref, shift_ref, scale_ref, rows_ref, normed_ref):
    x = x_ref[0]
    moved, there = moved_ref[...], there_ref[...]
    low = jnp.where(x == 0, moved, there)
    high = jnp.where(x == 0, there, moved)
    first = jnp.concatenate([low[:, :HALF], high[:, :HALF]], axis=1)
    second = jnp.concatenate([low[:, HALF:], high[:, HALF:]], axis=1)
    own = jnp.where(x == 0, first, second)
    rows_ref[...] = own
    values = jnp.concatenate([own, jnp.where(x == 0, second, first)], axis=0)
    normed_ref[...] = norm_regroup(values.astype(jnp.float32), shift_ref[...], scale_ref[...])


def same_place():
    place_r = lax.broadcasted_iota(jnp.int32, (TOK, 2 * TOK), 0) % 8
    place_c = lax.broadcasted_iota(jnp.int32, (TOK, 2 * TOK), 1) % 8
    return place_r == place_c


def temporal_kernel(
    normed_ref, cos_ref, sin_ref, w_ref, give_ref, q_ref, k_ref, v_ref, mix_s
):
    rows = 2 * TOK
    normed = normed_ref[...]
    lane = lax.broadcasted_iota(jnp.int32, (rows, PAD), 1)
    front = lane % HEAD < HEAD // 2
    cos, sin = cos_ref[...], sin_ref[...]
    q = jnp.dot(normed, w_ref[:, :PAD], preferred_element_type=jnp.float32)
    k = jnp.dot(normed, w_ref[:, 512:D], preferred_element_type=jnp.float32)
    k = pltpu.roll(k, PAD - 64, 1)
    v = jnp.dot(normed, w_ref[:, 2 * D :], preferred_element_type=jnp.float32)
    v = v.astype(jnp.bfloat16)

    def rotate(a):
        other = jnp.where(front, pltpu.roll(a, PAD - HEAD // 2, 1), pltpu.roll(a, HEAD // 2, 1))
        return (a * cos + other * sin).astype(jnp.bfloat16)

    q, k = rotate(q), rotate(k)
    q_ref[...] = q[:TOK]
    k_ref[...] = k
    v_ref[...] = v
    attend(q[TOK:], k, v, mix_s, 0, TOK, same_place())
    give_ref[...] = regroup(mix_s[...], pltpu.roll)[:, :HALF].astype(jnp.bfloat16)


def temporal_own_kernel(q_ref, k_ref, v_ref, keep_ref, mix_s):
    attend(q_ref[...], k_ref[...], v_ref[...], mix_s, 0, TOK, same_place())
    keep_ref[...] = regroup(mix_s[...], pltpu.roll)[:, :HALF].astype(jnp.bfloat16)


def result_kernel(x_ref, own_ref, got_ref, rows_ref, gate_ref, w_ref, out_ref):
    added = mixed_dot(x_ref[0], own_ref[...], got_ref[...], w_ref, D, D)
    out_ref[...] = (rows_ref[...].astype(jnp.float32) + gate_ref[...] * added).astype(jnp.bfloat16)


VMEM_LIMIT = 32 * 2**20
VMEM = pl.BlockSpec(memory_space=pltpu.VMEM)
SMEM = pl.BlockSpec(memory_space=pltpu.SMEM)


def b16(*shape):
    return jax.ShapeDtypeStruct(shape, jnp.bfloat16)


def run(kernel, outs, specs, scratch, name, *operands):
    return pl.pallas_call(
        kernel,
        out_shape=outs,
        in_specs=specs,
        out_specs=jax.tree.map(lambda _: VMEM, outs),
        scratch_shapes=scratch,
        compiler_params=pltpu.CompilerParams(vmem_limit_bytes=VMEM_LIMIT),
        name=name,
    )(*operands)


def on_device(tokens, anchor, positions, w_spatial, w_temporal, mod_shift, mod_scale, mod_gate):
    index = lax.axis_index("frame")
    z, x, core = index // 4, index // 2 % 2, index % 2
    root = anchor[0]
    root_z, root_x, root_core = root // 4, root // 2 % 2, root % 2

    x_arg = jnp.reshape(x, (1,)).astype(jnp.int32)

    own = tokens[0]
    s_rows, s_got = swap_rows(w_spatial, x)

    def rows_for(x_at, core_at):
        return lax.dynamic_slice_in_dim(own, (2 * x_at + core_at) * 32, 32, 0)

    quarter = jnp.where(
        root_x == x,
        jnp.where(root_core == core, rows_for(x, core), swap(rows_for(x, 1 - core), CORE)),
        jnp.where(
            root_core == core,
            swap(rows_for(1 - x, core), X_LO),
            swap(rows_for(1 - x, 1 - core), X_CORE),
        ),
    )
    side = jnp.where(z % 2 == 0, 1, -1)
    t_slab = temporal_slab(w_temporal, x, s_got)
    s_own = ring_gather(spatial_slabs(s_rows, s_got, quarter, x), z, side)
    s_other = [swap(full, CORE) for full in s_own]
    own = after(own, quarter)

    def chosen(full):
        return lax.dynamic_slice(full, (root_z, 0, D), (1, 72, 256))[0]

    near = jnp.concatenate([chosen(s_own[0]), chosen(s_own[1])], axis=1)
    pairs = jnp.concatenate([near, swap(near, X_LO)], axis=0)
    anchor_rows = jnp.concatenate([pairs, swap(pairs, CORE)], axis=0)

    pair = ordered(x, own, swap(own, X_LO), 0)
    normed = regroup(modulated_norm(pair, mod_shift[0], mod_scale[0]), jnp.roll)
    tokens_half = halves(pair, x)[0]
    gate_half = halves(mod_gate[:1], x)[0]

    w_qk, w_vo = [both_cores(s_own[i], s_other[i], core) for i in range(2)]
    t_slab = after(t_slab, near)
    t_own = put(jnp.zeros((8,) + t_slab.shape, t_slab.dtype), t_slab, z)
    even, odd = swap(t_slab, Z_EVEN), swap(t_slab, Z_ODD)

    qk, v = run(
        project_kernel, (b16(2 * TOK, D), b16(2 * TOK, PAD)), [VMEM] * 3, [], "project",
        normed, w_qk, w_vo,
    )
    mix = run(
        spatial_kernel,
        b16(2 * TOK, HALF),
        [VMEM] * 7,
        [pltpu.VMEM((2 * TOK, PAD), jnp.float32)],
        "spatial",
        qk,
        v,
        anchor_rows,
        mod_shift[:1],
        mod_scale[:1],
        w_qk,
        w_vo,
    )

    def round_with(step, work, even, odd, t_own):
        work, even, odd = lax.optimization_barrier((work, even, odd))
        t_own = put(put(t_own, even, z + side * step), odd, z - side * step)
        return work, swap(odd, Z_EVEN), swap(even, Z_ODD), t_own

    mix, even, odd, t_own = round_with(1, mix, even, odd, t_own)
    hidden = run(
        hidden_kernel,
        b16(TOK, D),
        [SMEM] + [VMEM] * 5,
        [],
        "hidden",
        x_arg,
        mix,
        swap(mix, X_LO),
        tokens_half,
        gate_half,
        w_vo,
    )

    hidden, even, odd, t_own = round_with(2, hidden, even, odd, t_own)
    moved = lax.all_to_all(
        hidden.reshape(16, 8, D),
        "frame",
        split_axis=0,
        concat_axis=0,
        axis_index_groups=SAME_X,
        tiled=True,
    ).reshape(TOK, D)
    moved, even, odd = lax.optimization_barrier((moved, even, odd))
    t_own = put(put(t_own, even, z + side * 3), odd, z - side * 3)
    there = swap(moved, X_LO)
    cut = 1408
    last = jnp.concatenate([swap(odd[:, :cut], Z_EVEN), swap(even[:, cut:], Z_ODD)], axis=1)
    t_other = swap(t_own, CORE)
    t_w = both_cores(put(t_own, last, z + 4), put(t_other, swap(last, CORE), z + 4), core)

    half_size = HEAD // 2
    freqs = 10000.0 ** (-jnp.arange(half_size, dtype=jnp.float32) / half_size)
    by_x = positions.reshape(8, 2, 2).transpose(1, 0, 2)
    by_row = jnp.where(x == 0, by_x, by_x[::-1]).reshape(32)
    angles = by_row.astype(jnp.float32)[:, None] * freqs[None, :]
    cosine, sine = jnp.cos(angles), jnp.sin(angles)

    def spread(first, second):
        table = jnp.tile(jnp.concatenate([first, second], axis=1), (1, HEADS // 2))
        table = jnp.pad(table, ((0, 0), (0, PAD - HALF)))
        return jnp.broadcast_to(table[:, None], (32, 8, PAD)).reshape(2 * TOK, PAD)

    rows, t_normed = run(
        rows_kernel,
        (b16(TOK, D), b16(2 * TOK, D)),
        [SMEM] + [VMEM] * 4,
        [],
        "rows",
        x_arg,
        moved,
        there,
        mod_shift[1:],
        mod_scale[1:],
    )
    give, t_q, t_k, t_v = run(
        temporal_kernel,
        (b16(TOK, HALF), b16(TOK, PAD), b16(2 * TOK, PAD), b16(2 * TOK, PAD)),
        [VMEM] * 4,
        [pltpu.VMEM((TOK, PAD), jnp.float32)],
        "temporal",
        t_normed,
        spread(cosine, cosine),
        spread(-sine, sine),
        t_w,
    )
    keep = run(
        temporal_own_kernel,
        b16(TOK, HALF),
        [VMEM] * 3,
        [pltpu.VMEM((TOK, PAD), jnp.float32)],
        "temporal_own",
        t_q,
        t_k,
        t_v,
    )
    result = run(
        result_kernel,
        b16(TOK, D),
        [SMEM] + [VMEM] * 5,
        [],
        "result",
        x_arg,
        keep,
        swap(give, X_LO),
        rows,
        mod_gate[1:],
        t_w,
    )
    back = lax.all_to_all(
        result.reshape(16, 8, D),
        "frame",
        split_axis=0,
        concat_axis=0,
        axis_index_groups=SAME_X,
        tiled=True,
    )
    return back.reshape(1, TOK, D)


def solution(mesh):
    placed = (
        P(("batch", "frame"), None, None),
        P("batch"),
        P("batch"),
        P(None, "frame", None),
        P(None, "frame", None),
        P("batch", None),
        P("batch", None),
        P("batch", None),
    )
    return jax.shard_map(
        on_device,
        mesh=mesh,
        in_specs=placed,
        out_specs=P(("batch", "frame"), None, None),
        check_vma=False,
    )
```
